256 devices in a mesh: grp: 2 (over core), seq: 16 (over x, y), head: 8 (over z).
Axes of the slice: x: 4, y: 4, z: 8, core: 2. Of those that a mesh axis runs over, the one named last changes fastest.
Arguments:
- prompt_q: bfloat16 [2, 3072, 8192], P('grp', 'seq', 'head'), may hold values from -8 to 8
- prompt_kv: bfloat16 [2, 3072, 2048], P('grp', 'seq', 'head'), may hold values from -24 to 24
- sectioned: bfloat16 [2, 512, 32, 2048], P('grp', 'seq', None, 'head'), may hold values from -6 to 6
- handoff_dest: int32 [2, 512, 1], P('grp', 'seq'), may hold values from 0 to 15; in each aligned block of 32 rows (0 to 31, 32 to 63, ..., all dimensions but the last counted through in order) at most 4 rows name the same one
- dec_q: bfloat16 [2, 32, 2, 8192], P('grp', 'seq', None, 'head'), may hold values from -8 to 8
- dec_new: bfloat16 [2, 32, 2, 2048], P('grp', 'seq', None, 'head'), may hold values from -24 to 24
- cache: bfloat16 [2, 32, 1024, 2048], P('grp', 'seq', None, 'head'), may hold values from -24 to 24
- cache_len: int32 [2, 32], P('grp', 'seq'), may hold values from 1 to 1024, 16384 in all within a row
- output_weight: bfloat16 [8192, 8192], P('head', 'seq'), may hold values from -0.09375 to 0.09375
Outputs:
- prompt_attn: bfloat16 [2, 3072, 8192], P('grp', 'seq', 'head')
- arrived: bfloat16 [2, 1024, 32, 2048], P('grp', 'seq', None, 'head')
- decode_out: bfloat16 [2, 64, 8192], P('grp', 'head', 'seq')
The draws below stay inside these ranges and needn't reach their ends.
Inputs may be any that keep to these rules, and one draw needn't show every extreme that they name: `handoff_dest`: among the rows of one device, at most 4 name the same shard, a bound that some block reaches of them.
All inputs are finite; a program needn't handle non-finite values. No bound on the sum of `cache_len` on one device may be relied on, other than what follows from the above.
Results may differ from the reference program's by a relative error of at most 0.019.
Values may be sent and summed in bfloat16 or wider, within the bound.
No kernel may reach another device: no remote copies, remote signals or barrier semaphores. Data moves between devices by JAX's collectives and lax.ppermute only.
A program may use at most 64 MiB of HBM per device.

```python
import math
import jax
import jax.numpy as jnp
import numpy as np
from jax import lax

MODEL_WIDTH = 8192
KEY_HEADS = 8
QUERY_PER_KEY = 8
HEAD_WIDTH = 128
P_DEV = 192
CACHE_POSITIONS = 1024
DECODE_STEPS = 2
SECTION_BLOCKS = 32
BLOCK_POSITIONS = 32
PROMPT_LENGTH = 3072
DECODE_REQUESTS = 32
MOST_SEND_BLOCKS = 4
N_GRP = 2
N_SEQ = 16


def draw_prompt_kv(key, part):
    key = jax.random.fold_in(key, 11)
    complete_shape = (N_GRP, PROMPT_LENGTH, KEY_HEADS, 2, HEAD_WIDTH)
    half_scale = jnp.array([1.0, 4.0], jnp.float32)[:, None]
    unprojected_values = jnp.clip(jax.random.normal(key, complete_shape, jnp.float32), -6.0, 6.0) * half_scale
    return unprojected_values.reshape(N_GRP, PROMPT_LENGTH, KEY_HEADS * 2 * HEAD_WIDTH).astype(jnp.bfloat16)


def draw_prompt_q(key, part):
    key = jax.random.fold_in(key, 12)
    complete_shape = (N_GRP, PROMPT_LENGTH, KEY_HEADS * QUERY_PER_KEY, HEAD_WIDTH)
    unprojected_values = jnp.clip(jax.random.normal(key, complete_shape, jnp.float32), -6.0, 6.0)
    return unprojected_values.reshape(N_GRP, PROMPT_LENGTH, KEY_HEADS * QUERY_PER_KEY * HEAD_WIDTH).astype(jnp.bfloat16)


def draw_cache(key, part):
    key = jax.random.fold_in(key, 13)
    complete_shape = (N_GRP, DECODE_REQUESTS, CACHE_POSITIONS, KEY_HEADS, 2, HEAD_WIDTH)
    half_scale = jnp.array([1.0, 4.0], jnp.float32)[:, None]
    unprojected_values = jnp.clip(jax.random.normal(key, complete_shape, jnp.float32), -6.0, 6.0) * half_scale
    return unprojected_values.reshape(N_GRP, DECODE_REQUESTS, CACHE_POSITIONS, KEY_HEADS * 2 * HEAD_WIDTH).astype(jnp.bfloat16)


def draw_dec_new(key, part):
    key = jax.random.fold_in(key, 14)
    complete_shape = (N_GRP, DECODE_REQUESTS, DECODE_STEPS, KEY_HEADS, 2, HEAD_WIDTH)
    half_scale = jnp.array([1.0, 4.0], jnp.float32)[:, None]
    unprojected_values = jnp.clip(jax.random.normal(key, complete_shape, jnp.float32), -6.0, 6.0) * half_scale
    return unprojected_values.reshape(N_GRP, DECODE_REQUESTS, DECODE_STEPS, KEY_HEADS * 2 * HEAD_WIDTH).astype(jnp.bfloat16)


def draw_dec_q(key, part):
    key = jax.random.fold_in(key, 15)
    complete_shape = (N_GRP, DECODE_REQUESTS, DECODE_STEPS, KEY_HEADS * QUERY_PER_KEY, HEAD_WIDTH)
    unprojected_values = jnp.clip(jax.random.normal(key, complete_shape, jnp.float32), -6.0, 6.0)
    return unprojected_values.reshape(N_GRP, DECODE_REQUESTS, DECODE_STEPS, KEY_HEADS * QUERY_PER_KEY * HEAD_WIDTH).astype(jnp.bfloat16)


def block_scale(key, extent, pieces, smallest, largest):
    def one(axis_at, shards_of):
        steps = jax.random.uniform(jax.random.fold_in(jax.random.fold_in(key, 6), axis_at), (shards_of,), jnp.float32, smallest / len(pieces), largest / len(pieces))
        return jnp.repeat(jnp.exp(steps), extent[axis_at] // shards_of).reshape((-1,) + (1,) * (len(extent) - axis_at - 1))

    factor_of = one(*pieces[0])
    for cut in pieces[1:]:
        factor_of = factor_of * one(*cut)
    return factor_of


def split_up(count, total, bound, lean):
    loads = [(1 << 20) // math.isqrt(grade ** lean) + 1 for grade in range(2, count + 1)]
    surplus, holding = total - bound - (count - 1), [1] * (count - 1)
    while surplus > 0:
        free = [i for i in range(count - 1) if holding[i] < bound]
        whole, remaining = sum([loads[i] for i in free]), surplus
        for i in free:
            more = min(bound - holding[i], max(1, remaining * loads[i] // whole), surplus)
            holding[i] = holding[i] + more
            surplus = surplus - more
    return np.array([bound] + holding)


def uneven(own_key, number_of, total, most, lean):
    if number_of == 2:
        one = jax.random.randint(own_key, (), max(1, total - most), min(most, total - 1) + 1)
        return jnp.stack([one, total - one])
    tallies = jnp.asarray(split_up(number_of, total, most, lean), jnp.int32)
    twos = (number_of - 1) // 2
    donor, receiver = tallies[1:1 + 2 * twos:2], tallies[2:2 + 2 * twos:2]
    margin = jnp.minimum(donor - 1, most - receiver)
    passed = jax.random.randint(jax.random.fold_in(own_key, 1), (twos,), 0, 1 << 20) % (margin + 1)
    tallies = tallies.at[1:1 + 2 * twos:2].set(donor - passed).at[2:2 + 2 * twos:2].set(receiver + passed)
    return tallies[jax.random.permutation(jax.random.fold_in(own_key, 2), number_of)]


def deal_out(own_key, own, number, rows, number_of, top, limit, lean):
    sequence = jax.random.permutation(own_key, number_of)
    packed, usual = load_shares(number_of, rows * top, limit, lean, True), load_shares(number_of, rows * top, limit, lean, False)
    places = jnp.arange(number_of)

    def named(lengths, offset_by):
        used = int((lengths > 0).sum())
        fixed = max(1, used // 4)
        shifted = fixed + (places - fixed + offset_by * (used - fixed)) % max(1, number_of - fixed)
        return jnp.zeros((number_of,), jnp.int32).at[sequence[jnp.where(places < fixed, places, shifted)]].set(jnp.asarray(lengths, jnp.int32))

    lengths = jnp.where(number % 4 == 0, named(packed, number // 4), named(usual, number - number // 4 - 1))
    mixed = jax.random.permutation(jax.random.fold_in(own, 3), number_of)
    donor, receiver = mixed[0:number_of // 2 * 2:2], mixed[1:number_of // 2 * 2:2]
    slack = jnp.minimum(lengths[donor] - 1, limit - lengths[receiver]) // 2
    slack = jnp.where((donor == sequence[0]) | (receiver == sequence[0]) | (lengths[receiver] == 0), 0, jnp.maximum(slack, 0))
    shifted = jax.random.randint(jax.random.fold_in(own, 4), (number_of // 2,), 0, 1 << 20) % (slack + 1)
    lengths = lengths.at[donor].add(-shifted).at[receiver].add(shifted)
    members = jnp.searchsorted(jnp.cumsum(lengths), jnp.arange(rows * top), side="right").astype(jnp.int32)
    grid = members.reshape(top, rows).T
    grid = grid[jax.random.permutation(jax.random.fold_in(own, 1), rows)]
    offset_by = jax.random.randint(jax.random.fold_in(own, 2), (rows, 1), 0, top)
    return jnp.take_along_axis(grid, (jnp.arange(top)[None, :] + offset_by) % top, axis=1)


def load_shares(number_of, total, reach, lean, full):
    weights = [(1 << 20) // math.isqrt(rank ** lean) + 1 for rank in range(1, number_of + 1)]
    largest = reach if full else min(reach, max(-(-total // number_of), total * weights[0] // sum(weights)))
    least = 1 if total - largest >= number_of - 1 else 0
    holding, spare = [largest] + [least] * (number_of - 1), total - largest - least * (number_of - 1)
    while spare > 0:
        candidates = [i for i in range(1, number_of) if holding[i] < largest] or [i for i in range(1, number_of) if holding[i] < reach]
        pool, left = sum([weights[i] for i in candidates]), spare
        for i in candidates:
            addition = min(reach - holding[i], max(1, left * weights[i] // pool), spare)
            holding[i] = holding[i] + addition
            spare = spare - addition
    return np.array(holding)


def centred(own_key, dims, deviation, reach, pieces=(), kind=jnp.bfloat16):
    values = deviation * jax.random.normal(own_key, dims, jnp.float32)
    if pieces:
        values = values * block_scale(own_key, dims, pieces, -0.22, 0.18)
    return jnp.clip(values, -reach, reach).astype(kind)


def setup_inputs(seed: int = 0) -> dict:
    arg_keys = jax.random.split(jax.random.key(seed), 10)
    prompt_q = draw_prompt_q(jax.random.fold_in(arg_keys[9], 71), 0)
    prompt_kv = draw_prompt_kv(jax.random.fold_in(arg_keys[9], 71), 0)
    sectioned = centred(arg_keys[2], (N_GRP, N_SEQ * SECTION_BLOCKS, BLOCK_POSITIONS, KEY_HEADS * 2 * HEAD_WIDTH), 1.0, 6.0, ((0, 2), (1, 16), (3, 8)))
    handoff_dest_keys = jax.random.split(jax.random.fold_in(arg_keys[3], 1), N_GRP * (N_SEQ * SECTION_BLOCKS) // SECTION_BLOCKS)
    handoff_dest_turns = jax.random.permutation(jax.random.fold_in(arg_keys[3], 3), N_GRP * (N_SEQ * SECTION_BLOCKS) // SECTION_BLOCKS)
    handoff_dest = jax.vmap(lambda own, number: deal_out(jax.random.fold_in(arg_keys[3], 2), own, number, SECTION_BLOCKS, N_SEQ, 1, MOST_SEND_BLOCKS, 2))(handoff_dest_keys, handoff_dest_turns).reshape((N_GRP, N_SEQ * SECTION_BLOCKS, 1))
    dec_q = draw_dec_q(jax.random.fold_in(arg_keys[9], 71), 0)
    dec_new = draw_dec_new(jax.random.fold_in(arg_keys[9], 71), 0)
    cache = draw_cache(jax.random.fold_in(arg_keys[9], 71), 0)
    cache_len = jax.vmap(lambda own: uneven(own, DECODE_REQUESTS, DECODE_REQUESTS * CACHE_POSITIONS // 2, CACHE_POSITIONS, 2))(jax.random.split(arg_keys[7], N_GRP)).reshape((N_GRP, DECODE_REQUESTS)).astype(jnp.int32)
    output_weight = centred(arg_keys[8], (KEY_HEADS * QUERY_PER_KEY * HEAD_WIDTH, MODEL_WIDTH), (KEY_HEADS * QUERY_PER_KEY * HEAD_WIDTH // 2) ** -0.5, 0.09375, ((0, 8), (1, 16)))
    return dict(prompt_q=prompt_q, prompt_kv=prompt_kv, sectioned=sectioned, handoff_dest=handoff_dest, dec_q=dec_q, dec_new=dec_new, cache=cache, cache_len=cache_len, output_weight=output_weight)


def prefill_group(query_of_group, group_pairings):
    score_scale = 1.0 / math.sqrt(HEAD_WIDTH)
    query_head = query_of_group.reshape(PROMPT_LENGTH, KEY_HEADS, QUERY_PER_KEY, HEAD_WIDTH).transpose(1, 0, 2, 3)
    key_value_head = group_pairings.reshape(PROMPT_LENGTH, KEY_HEADS, 2, HEAD_WIDTH).transpose(1, 0, 2, 3)
    key_pos = jnp.arange(PROMPT_LENGTH, dtype=jnp.int32)

    def per_head(inputs):
        head_queries, head_pairs = inputs
        head_keys = head_pairs[:, 0, :].astype(jnp.float32)
        head_values = head_pairs[:, 1, :].astype(jnp.float32)
        query_blocks = head_queries.reshape(N_SEQ, P_DEV, QUERY_PER_KEY, HEAD_WIDTH)

        def per_block(block_inputs):
            query_block, block_index = block_inputs
            scores = jnp.einsum('pqd,kd->qpk', query_block.astype(jnp.float32), head_keys) * score_scale
            query_pos = block_index * P_DEV + jnp.arange(P_DEV, dtype=jnp.int32)
            visible = key_pos[None, :] <= query_pos[:, None]
            scores = jnp.where(visible[None], scores, -jnp.inf)
            row_max = lax.optimization_barrier(jnp.max(scores, axis=-1, keepdims=True))
            weights = jnp.exp(scores - row_max)
            weight_sum = lax.optimization_barrier(jnp.sum(weights, axis=-1))
            rounded = lax.optimization_barrier(weights.astype(jnp.bfloat16))
            weighted = jnp.einsum('qpk,kd->pqd', rounded.astype(jnp.float32), head_values)
            return weighted / weight_sum.T[:, :, None]
        block_outputs = lax.map(per_block, (query_blocks, jnp.arange(N_SEQ, dtype=jnp.int32)))
        return block_outputs.reshape(PROMPT_LENGTH, QUERY_PER_KEY, HEAD_WIDTH)
    head_split_output = lax.map(per_head, (query_head, key_value_head))
    return head_split_output.transpose(1, 0, 2, 3).reshape(PROMPT_LENGTH, KEY_HEADS * QUERY_PER_KEY * HEAD_WIDTH).astype(jnp.bfloat16)

def decode_group(query_of_group, fresh_group_entries, cache_of_group, group_lengths, output_weight):
    score_scale = 1.0 / math.sqrt(HEAD_WIDTH)
    query_rows = query_of_group.reshape(DECODE_REQUESTS, DECODE_STEPS, KEY_HEADS, QUERY_PER_KEY, HEAD_WIDTH).astype(jnp.float32)
    cache_written = cache_of_group.reshape(DECODE_REQUESTS, CACHE_POSITIONS, KEY_HEADS, 2, HEAD_WIDTH).astype(jnp.float32)
    latest_entry = fresh_group_entries.reshape(DECODE_REQUESTS, DECODE_STEPS, KEY_HEADS, 2, HEAD_WIDTH).astype(jnp.float32)
    cache_scores = jnp.einsum('rthqd,rchd->rhqtc', query_rows, cache_written[:, :, :, 0, :]) * score_scale
    new_scores = jnp.einsum('rthqd,rshd->rhqts', query_rows, latest_entry[:, :, :, 0, :]) * score_scale
    live_mask = jnp.arange(CACHE_POSITIONS, dtype=jnp.int32)[None, :] < group_lengths[:, None]
    causal = jnp.arange(DECODE_STEPS, dtype=jnp.int32)[None, :] <= jnp.arange(DECODE_STEPS, dtype=jnp.int32)[:, None]
    cache_scores = jnp.where(live_mask[:, None, None, None, :], cache_scores, -jnp.inf)
    new_scores = jnp.where(causal[None, None, None], new_scores, -jnp.inf)
    row_max = jnp.maximum(lax.optimization_barrier(jnp.max(cache_scores, axis=-1)), lax.optimization_barrier(jnp.max(new_scores, axis=-1)))
    cache_weights = jnp.exp(cache_scores - row_max[..., None])
    new_weights = jnp.exp(new_scores - row_max[..., None])
    weight_sum = lax.optimization_barrier(jnp.sum(cache_weights, axis=-1)) + lax.optimization_barrier(jnp.sum(new_weights, axis=-1))
    cache_rounded = lax.optimization_barrier(cache_weights.astype(jnp.bfloat16))
    new_rounded = lax.optimization_barrier(new_weights.astype(jnp.bfloat16))
    weighted = jnp.einsum('rhqtc,rchd->rthqd', cache_rounded.astype(jnp.float32), cache_written[:, :, :, 1, :])
    weighted = weighted + jnp.einsum('rhqts,rshd->rthqd', new_rounded.astype(jnp.float32), latest_entry[:, :, :, 1, :])
    attention_output = (weighted / weight_sum.transpose(0, 3, 1, 2)[..., None]).astype(jnp.bfloat16)
    attention_output = attention_output.reshape(DECODE_REQUESTS * DECODE_STEPS, KEY_HEADS * QUERY_PER_KEY * HEAD_WIDTH)
    return jnp.dot(attention_output, output_weight, preferred_element_type=jnp.float32).astype(jnp.bfloat16)

def handoff(sectioned, handoff_dest):
    received_groups = []
    for target in range(N_GRP):
        source = N_GRP - 1 - target
        targets = handoff_dest[source, :, 0].reshape(N_SEQ, SECTION_BLOCKS)
        hit_table = (targets[:, :, None] == jnp.arange(N_SEQ, dtype=jnp.int32)[None, None, :]).astype(jnp.int32)
        running_count = jnp.cumsum(hit_table, axis=1).astype(jnp.int32) - 1
        block_rank = lax.optimization_barrier(jnp.sum(running_count * hit_table, axis=2)).astype(jnp.int32)
        slot_index = targets * (N_SEQ * MOST_SEND_BLOCKS) + jnp.arange(N_SEQ, dtype=jnp.int32)[:, None] * MOST_SEND_BLOCKS + block_rank
        slot_index = slot_index.reshape(N_SEQ * SECTION_BLOCKS).astype(jnp.int32)
        blank_block_pool = jnp.zeros((N_SEQ * N_SEQ * MOST_SEND_BLOCKS, BLOCK_POSITIONS, KEY_HEADS * 2 * HEAD_WIDTH), jnp.bfloat16)
        received_groups.append(blank_block_pool.at[slot_index].set(sectioned[source]))
    return jnp.stack(received_groups)

def reference(prompt_q, prompt_kv, sectioned, handoff_dest, dec_q, dec_new, cache, cache_len, output_weight):
    prompt_attn = jnp.stack([prefill_group(prompt_q[group_id], prompt_kv[group_id]) for group_id in range(N_GRP)])
    arrived = handoff(sectioned, handoff_dest)
    decode_out = jnp.stack([decode_group(dec_q[group_id], dec_new[group_id], cache[group_id], cache_len[group_id], output_weight) for group_id in range(N_GRP)])
    return (prompt_attn, arrived, decode_out)
```

```python
import math

import jax
import jax.numpy as jnp
from jax import lax
from jax.experimental import pallas as pl
from jax.experimental.pallas import tpu as pltpu
from jax.sharding import PartitionSpec as P

QUERY_PER_KEY = 8
HEAD_WIDTH = 128
SCORE_SCALE = 1.0 / math.sqrt(HEAD_WIDTH)
EXP2_SCALE = SCORE_SCALE * math.log2(math.e)
LOWEST = -3.0e38
SLOTS = 4
BLOCKS_PER_CHUNK = 4

NT = (((1,), (1,)), ((), ()))
NN = (((1,), (0,)), ((), ()))


def dot(a, b, dims=NN):
    return lax.dot_general(a, b, dims, preferred_element_type=jnp.float32)


def prompt_kernel(shard_ref, q_ref, kv_ref, out_ref, val, acc, top):
    shard = shard_ref[0]
    length = q_ref.shape[0]
    chunk = BLOCKS_PER_CHUNK * length
    val[:, HEAD_WIDTH:] = jnp.ones((chunk, HEAD_WIDTH), jnp.bfloat16)

    def step(at, masked, first):
        kv = kv_ref[pl.ds(at * BLOCKS_PER_CHUNK, BLOCKS_PER_CHUNK)].reshape(chunk, 2 * HEAD_WIDTH)
        keys = kv[:, :HEAD_WIDTH]
        val[:, :HEAD_WIDTH] = kv[:, HEAD_WIDTH:]
        if masked:
            key_pos = at * chunk + lax.broadcasted_iota(jnp.int32, (length, chunk), 1)
            query_pos = shard * length + lax.broadcasted_iota(jnp.int32, (length, chunk), 0)
            visible = key_pos <= query_pos
        for head in range(QUERY_PER_KEY):
            rows = pl.ds(head * length, length)
            q = q_ref[:, head * HEAD_WIDTH : (head + 1) * HEAD_WIDTH]
            scores = dot(q, keys, NT)
            if masked:
                scores = jnp.where(visible, scores, LOWEST)
            peak = jnp.max(scores, axis=1, keepdims=True)
            if not first:
                old = top[rows, :]
                peak = jnp.maximum(old[:, :1], peak)
            weights = jnp.exp2((scores - peak) * EXP2_SCALE).astype(jnp.bfloat16)
            part = dot(weights, val[...])
            if not first:
                part = acc[rows, :] * jnp.exp2((old[:, :1] - peak) * EXP2_SCALE) + part
            if masked:
                out_ref[:, head * HEAD_WIDTH : (head + 1) * HEAD_WIDTH] = (
                    part[:, :HEAD_WIDTH] / part[:, HEAD_WIDTH:]
                ).astype(jnp.bfloat16)
            else:
                acc[rows, :] = part
                top[rows, :] = jnp.broadcast_to(peak, (length, HEAD_WIDTH))

    last = shard // BLOCKS_PER_CHUNK

    @pl.when(last == 0)
    def _():
        step(0, True, True)

    @pl.when(last > 0)
    def _():
        step(0, False, True)

        @pl.loop(1, last)
        def _(at):
            step(at, False, False)

        step(last, True, False)


def prompt_attention(shard, q, kv):
    length = q.shape[0]
    rows = QUERY_PER_KEY * length
    chunk = BLOCKS_PER_CHUNK * length
    whole = pl.BlockSpec(memory_space=pltpu.VMEM)
    return pl.pallas_call(
        prompt_kernel,
        out_shape=jax.ShapeDtypeStruct(q.shape, jnp.bfloat16),
        in_specs=[pl.BlockSpec(memory_space=pltpu.SMEM), whole, whole],
        out_specs=whole,
        scratch_shapes=[
            pltpu.VMEM((chunk, 2 * HEAD_WIDTH), jnp.bfloat16),
            pltpu.VMEM((rows, 2 * HEAD_WIDTH), jnp.float32),
            pltpu.VMEM((rows, HEAD_WIDTH), jnp.float32),
        ],
        compiler_params=pltpu.CompilerParams(vmem_limit_bytes=24 << 20),
        cost_estimate=pl.CostEstimate(
            flops=6 * rows * 16 * length * HEAD_WIDTH,
            bytes_accessed=2 * (2 * q.size + kv.size),
            transcendentals=rows * 16 * length,
        ),
        name="prompt_attention",
    )(shard, q, kv)


def decode_kernel(len_ref, q_ref, new_ref, cache_ref, out_ref, q_rows, fresh, out_rows):
    requests, steps, _ = q_ref.shape
    capacity = cache_ref.shape[1]
    rows = QUERY_PER_KEY * steps
    for req in range(requests):
        for head in range(QUERY_PER_KEY):
            q_rows[head * steps : (head + 1) * steps, :] = q_ref[
                req, :, head * HEAD_WIDTH : (head + 1) * HEAD_WIDTH
            ].astype(jnp.float32)
        q = q_rows[...].astype(jnp.bfloat16)
        fresh[...] = jnp.zeros_like(fresh)
        fresh[:steps, :] = new_ref[req].astype(jnp.float32)
        new = fresh[...].astype(jnp.bfloat16)
        kv = cache_ref[req]
        scores = dot(q, kv[:, :HEAD_WIDTH], NT)
        position = lax.broadcasted_iota(jnp.int32, (rows, capacity), 1)
        scores = jnp.where(position < len_ref[0, req], scores, LOWEST)
        new_scores = dot(q, new[:, :HEAD_WIDTH], NT)
        width = new.shape[0]
        new_pos = lax.broadcasted_iota(jnp.int32, (rows, width), 1)
        step = lax.broadcasted_iota(jnp.int32, (rows, width), 0) % steps
        new_scores = jnp.where(new_pos <= step, new_scores, LOWEST)
        peak = jnp.maximum(
            jnp.max(scores, axis=1, keepdims=True), jnp.max(new_scores, axis=1, keepdims=True)
        )
        weights = jnp.exp2((scores - peak) * EXP2_SCALE)
        new_weights = jnp.exp2((new_scores - peak) * EXP2_SCALE)
        total = jnp.sum(weights, axis=1, keepdims=True) + jnp.sum(new_weights, axis=1, keepdims=True)
        summed = dot(weights.astype(jnp.bfloat16), kv[:, HEAD_WIDTH:])
        summed = summed + dot(new_weights.astype(jnp.bfloat16), new[:, HEAD_WIDTH:])
        result = summed / total
        for head in range(QUERY_PER_KEY):
            out_rows[
                req * steps : (req + 1) * steps, head * HEAD_WIDTH : (head + 1) * HEAD_WIDTH
            ] = result[head * steps : (head + 1) * steps, :]
    out_ref[...] = out_rows[...].astype(jnp.bfloat16)


def decode_attention(lengths, q, new, cache):
    requests, steps, width = q.shape
    whole = pl.BlockSpec(memory_space=pltpu.VMEM)
    return pl.pallas_call(
        decode_kernel,
        out_shape=jax.ShapeDtypeStruct((requests * steps, width), jnp.bfloat16),
        in_specs=[pl.BlockSpec(memory_space=pltpu.SMEM), whole, whole, whole],
        out_specs=whole,
        scratch_shapes=[
            pltpu.VMEM((QUERY_PER_KEY * steps, HEAD_WIDTH), jnp.float32),
            pltpu.VMEM((HEAD_WIDTH, 2 * HEAD_WIDTH), jnp.float32),
            pltpu.VMEM((requests * steps, width), jnp.float32),
        ],
        compiler_params=pltpu.CompilerParams(vmem_limit_bytes=16 << 20),
        cost_estimate=pl.CostEstimate(
            flops=4 * q.size * cache.shape[1], bytes_accessed=2 * cache.size, transcendentals=0
        ),
        name="decode_attention",
    )(lengths, q, new, cache)


def place_kernel(dest_ref, blocks_ref, out_ref, count):
    targets = out_ref.shape[0] // SLOTS
    for target in range(targets):
        count[target] = 0
    out_ref[...] = jnp.zeros_like(out_ref)

    @pl.loop(0, blocks_ref.shape[0])
    def _(block):
        target = dest_ref[0, block]
        rank = count[target]
        count[target] = rank + 1
        slot = jnp.minimum(target * SLOTS + rank, targets * SLOTS - 1)
        out_ref[pl.ds(slot, 1)] = blocks_ref[pl.ds(block, 1)]


def place_blocks(dest, blocks, targets):
    whole = pl.BlockSpec(memory_space=pltpu.VMEM)
    shape = (targets * SLOTS,) + blocks.shape[1:]
    return pl.pallas_call(
        place_kernel,
        out_shape=jax.ShapeDtypeStruct(shape, blocks.dtype),
        in_specs=[pl.BlockSpec(memory_space=pltpu.SMEM), whole],
        out_specs=whole,
        scratch_shapes=[pltpu.SMEM((targets,), jnp.int32)],
        compiler_params=pltpu.CompilerParams(vmem_limit_bytes=16 << 20),
        cost_estimate=pl.CostEstimate(flops=0, bytes_accessed=6 * blocks.size, transcendentals=0),
        name="place_blocks",
    )(dest, blocks)


def project_kernel(rows_ref, weight_ref, out_ref, rows):
    sources, height, _ = rows_ref.shape
    for source in range(sources):
        rows[source * height : (source + 1) * height, :] = rows_ref[source].astype(jnp.float32)
    out_ref[...] = dot(rows[...].astype(jnp.bfloat16), weight_ref[...]).astype(jnp.bfloat16)


def project(rows, weight):
    sources, height, width = rows.shape
    whole = pl.BlockSpec(memory_space=pltpu.VMEM)
    return pl.pallas_call(
        project_kernel,
        out_shape=jax.ShapeDtypeStruct((sources * height, weight.shape[1]), jnp.bfloat16),
        in_specs=[whole, whole],
        out_specs=whole,
        scratch_shapes=[pltpu.VMEM((sources * height, width), jnp.float32)],
        compiler_params=pltpu.CompilerParams(vmem_limit_bytes=16 << 20),
        cost_estimate=pl.CostEstimate(
            flops=2 * sources * height * weight.size, bytes_accessed=2 * weight.size, transcendentals=0
        ),
        name="project",
    )(rows, weight)


def per_device(
    prompt_q, prompt_kv, sectioned, handoff_dest, dec_q, dec_new, cache, cache_len, output_weight
):
    shards = lax.axis_size("seq")
    shard = lax.axis_index("seq").reshape(1)
    swap = [(0, 1), (1, 0)]

    spread = jnp.broadcast_to(prompt_kv, (shards,) + prompt_kv.shape[1:])
    all_kv = lax.all_to_all(spread, "seq", 0, 0, tiled=True)
    prompt_attn = prompt_attention(shard, prompt_q[0], all_kv)

    other_dest = lax.ppermute(handoff_dest.reshape(1, -1), "grp", swap)
    other_blocks = lax.ppermute(sectioned[0], "grp", swap)
    outgoing = place_blocks(other_dest, other_blocks, shards)
    arrived = lax.all_to_all(outgoing, "seq", 0, 0, tiled=True)

    rows = decode_attention(cache_len, dec_q[0], dec_new[0], cache[0])
    rows = jnp.broadcast_to(rows[None], (shards,) + rows.shape)
    rows = lax.all_to_all(rows, "seq", 0, 0, tiled=True)
    partial = project(rows, output_weight)
    ranks = lax.axis_size("head")
    parts = lax.all_to_all(
        partial.reshape(ranks, partial.shape[0] // ranks, partial.shape[1]), "head", 0, 0, tiled=True
    )
    decode_out = jnp.sum(parts.astype(jnp.float32), axis=0).astype(jnp.bfloat16)
    return (prompt_attn[None], arrived[None], decode_out[None])


def solution(mesh):
    placed = (
        P("grp", "seq", "head"),
        P("grp", "seq", "head"),
        P("grp", "seq", None, "head"),
        P("grp", "seq", None),
        P("grp", "seq", None, "head"),
        P("grp", "seq", None, "head"),
        P("grp", "seq", None, "head"),
        P("grp", "seq"),
        P("head", "seq"),
    )
    return jax.shard_map(
        per_device,
        mesh=mesh,
        in_specs=placed,
        out_specs=(P("grp", "seq", "head"), P("grp", "seq", None, "head"), P("grp", "head", "seq")),
        check_vma=False,
    )
```

```python
import math

import jax
import jax.numpy as jnp
from jax import lax
from jax.experimental import pallas as pl
from jax.experimental.pallas import tpu as pltpu
from jax.sharding import PartitionSpec as P

QUERY_PER_KEY = 8
HEAD_WIDTH = 128
SCORE_SCALE = 1.0 / math.sqrt(HEAD_WIDTH)
EXP2_SCALE = SCORE_SCALE * math.log2(math.e)
LOWEST = -3.0e38
SLOTS = 4
SIDE = 4

NT = (((1,), (1,)), ((), ()))
NN = (((1,), (0,)), ((), ()))


def dot(a, b, dims=NN):
    return lax.dot_general(a, b, dims, preferred_element_type=jnp.float32)


def prompt_kernel(shard_ref, q_ref, *refs):
    near, far, out_ref, keys, val, acc, top = refs[:2], refs[2:4], *refs[4:]
    shard = shard_ref[0]
    my_row, my_col = shard // SIDE, shard % SIDE
    length = q_ref.shape[0]
    half = length // 2
    chunk = SIDE * length
    val[:, HEAD_WIDTH:] = jnp.ones((chunk, HEAD_WIDTH), jnp.bfloat16)

    def step(at, first):
        for col in range(SIDE):
            low = near[at // 2][at % 2 * SIDE + col, :half]
            high = far[col // 2][col % 2 * SIDE + at]
            for base, part in ((0, low), (half, high)):
                place = slice(col * length + base, col * length + base + half)
                keys[place, :] = part[:, :HEAD_WIDTH]
                val[place, :HEAD_WIDTH] = part[:, HEAD_WIDTH:]
        if first:
            spot = lax.broadcasted_iota(jnp.int32, (length, chunk), 1)
            col = spot // length
            key_pos = (my_col ^ (col ^ (col // 2))) * length + spot - col * length
            query_pos = my_col * length + lax.broadcasted_iota(jnp.int32, (length, chunk), 0)
            visible = key_pos <= query_pos
        for head in range(QUERY_PER_KEY):
            rows = pl.ds(head * length, length)
            q = q_ref[:, head * HEAD_WIDTH : (head + 1) * HEAD_WIDTH]
            scores = dot(q, keys[...], NT)
            if first:
                scores = jnp.where(visible, scores, LOWEST)
            peak = jnp.max(scores, axis=1, keepdims=True)
            if not first:
                old = top[rows, :]
                peak = jnp.maximum(old[:, :1], peak)
            weights = jnp.exp2((scores - peak) * EXP2_SCALE).astype(jnp.bfloat16)
            part = dot(weights, val[...])
            if not first:
                part = acc[rows, :] * jnp.exp2((old[:, :1] - peak) * EXP2_SCALE) + part
            acc[rows, :] = part
            top[rows, :] = jnp.broadcast_to(peak, (length, HEAD_WIDTH))

    step(0, True)
    for at in range(1, SIDE):
        pl.when((my_row ^ at ^ (at // 2)) < my_row)(lambda at=at: step(at, False))
    for head in range(QUERY_PER_KEY):
        rows = pl.ds(head * length, length)
        out_ref[:, head * HEAD_WIDTH : (head + 1) * HEAD_WIDTH] = (
            acc[rows, :HEAD_WIDTH] / acc[rows, HEAD_WIDTH:]
        ).astype(jnp.bfloat16)


def prompt_attention(shard, q, near, far):
    length = q.shape[0]
    rows = QUERY_PER_KEY * length
    chunk = SIDE * length
    whole = pl.BlockSpec(memory_space=pltpu.VMEM)
    return pl.pallas_call(
        prompt_kernel,
        out_shape=jax.ShapeDtypeStruct(q.shape, jnp.bfloat16),
        in_specs=[pl.BlockSpec(memory_space=pltpu.SMEM)] + [whole] * 5,
        out_specs=whole,
        scratch_shapes=[
            pltpu.VMEM((chunk, HEAD_WIDTH), jnp.bfloat16),
            pltpu.VMEM((chunk, 2 * HEAD_WIDTH), jnp.bfloat16),
            pltpu.VMEM((rows, 2 * HEAD_WIDTH), jnp.float32),
            pltpu.VMEM((rows, HEAD_WIDTH), jnp.float32),
        ],
        compiler_params=pltpu.CompilerParams(vmem_limit_bytes=24 << 20),
        cost_estimate=pl.CostEstimate(
            flops=6 * rows * 16 * length * HEAD_WIDTH,
            bytes_accessed=2 * (2 * q.size + 16 * length * 2 * HEAD_WIDTH),
            transcendentals=rows * 16 * length,
        ),
        name="prompt_attention",
    )(shard, q, *near, *far)


def first_kernel(len_ref, kv_ref, q_ref, new_ref, cache_ref, near_ref, far_ref, *scratch):
    kv, q_in, new_in, cache, q_rows, fresh, out_rows, packed, sems = scratch
    copies = [
        pltpu.make_async_copy(src, dst, sems.at[i])
        for i, (src, dst) in enumerate(
            ((cache_ref, cache), (q_ref, q_in), (new_ref, new_in), (kv_ref, kv))
        )
    ]
    for copy in copies:
        copy.start()
    requests, steps, _ = q_in.shape
    capacity = cache.shape[1]
    rows = QUERY_PER_KEY * steps
    half = far_ref.shape[0]
    fresh[...] = jnp.zeros_like(fresh)
    for copy in copies[1:]:
        copy.wait()
    near_ref[:half, :] = kv[:half, :]
    far_ref[...] = kv[half:, :]
    copies[0].wait()
    for req in range(requests):
        for head in range(QUERY_PER_KEY):
            q_rows[head * steps : (head + 1) * steps, :] = q_in[
                req, :, head * HEAD_WIDTH : (head + 1) * HEAD_WIDTH
            ].astype(jnp.float32)
        q = q_rows[...].astype(jnp.bfloat16)
        fresh[:steps, :] = new_in[req].astype(jnp.float32)
        new = fresh[...].astype(jnp.bfloat16)
        held = cache[req]
        scores = dot(q, held[:, :HEAD_WIDTH], NT)
        position = lax.broadcasted_iota(jnp.int32, (rows, capacity), 1)
        scores = jnp.where(position < len_ref[0, req], scores, LOWEST)
        new_scores = dot(q, new[:, :HEAD_WIDTH], NT)
        new_pos = lax.broadcasted_iota(jnp.int32, (rows, new.shape[0]), 1)
        step = lax.broadcasted_iota(jnp.int32, (rows, new.shape[0]), 0) % steps
        new_scores = jnp.where(new_pos <= step, new_scores, LOWEST)
        peak = jnp.maximum(
            jnp.max(scores, axis=1, keepdims=True), jnp.max(new_scores, axis=1, keepdims=True)
        )
        weights = jnp.exp2((scores - peak) * EXP2_SCALE)
        new_weights = jnp.exp2((new_scores - peak) * EXP2_SCALE)
        total = jnp.sum(weights, axis=1, keepdims=True) + jnp.sum(new_weights, axis=1, keepdims=True)
        summed = dot(weights.astype(jnp.bfloat16), held[:, HEAD_WIDTH:])
        summed = summed + dot(new_weights.astype(jnp.bfloat16), new[:, HEAD_WIDTH:])
        result = summed / total
        for head in range(QUERY_PER_KEY):
            out_rows[
                req * steps : (req + 1) * steps, head * HEAD_WIDTH : (head + 1) * HEAD_WIDTH
            ] = result[head * steps : (head + 1) * steps, :]
    height, wide = requests * steps, packed.shape[1]
    for piece in range(packed.shape[0] // height):
        packed[piece * height : (piece + 1) * height, :] = out_rows[
            :, piece * wide : (piece + 1) * wide
        ]
    near_ref[half:, :] = packed[...].astype(jnp.bfloat16)


def first_step(lengths, kv, q, new, cache):
    requests, steps, width = q.shape
    half, wide = kv.shape[0] // 2, kv.shape[1]
    height = requests * steps * width // wide
    whole = pl.BlockSpec(memory_space=pltpu.VMEM)
    far_off = pl.BlockSpec(memory_space=pl.ANY)
    return pl.pallas_call(
        first_kernel,
        out_shape=(
            jax.ShapeDtypeStruct((half + height, wide), jnp.bfloat16),
            jax.ShapeDtypeStruct((half, wide), jnp.bfloat16),
        ),
        in_specs=[pl.BlockSpec(memory_space=pltpu.SMEM)] + [far_off] * 4,
        out_specs=(whole, whole),
        scratch_shapes=[
            pltpu.VMEM(kv.shape, jnp.bfloat16),
            pltpu.VMEM(q.shape, jnp.bfloat16),
            pltpu.VMEM(new.shape, jnp.bfloat16),
            pltpu.VMEM(cache.shape, jnp.bfloat16),
            pltpu.VMEM((QUERY_PER_KEY * steps, HEAD_WIDTH), jnp.float32),
            pltpu.VMEM((HEAD_WIDTH, 2 * HEAD_WIDTH), jnp.float32),
            pltpu.VMEM((requests * steps, width), jnp.float32),
            pltpu.VMEM((height, wide), jnp.float32),
            pltpu.SemaphoreType.DMA((4,)),
        ],
        compiler_params=pltpu.CompilerParams(vmem_limit_bytes=60 << 20),
        cost_estimate=pl.CostEstimate(
            flops=4 * q.size * cache.shape[1], bytes_accessed=2 * cache.size, transcendentals=0
        ),
        name="first_step",
    )(lengths, kv, q, new, cache)


def place_kernel(dest_ref, blocks_ref, out_ref, count):
    targets = out_ref.shape[0] // SLOTS
    for target in range(targets):
        count[target] = 0
    out_ref[...] = jnp.zeros_like(out_ref)

    @pl.loop(0, blocks_ref.shape[0])
    def _(block):
        target = dest_ref[0, block]
        rank = count[target]
        count[target] = rank + 1
        slot = jnp.minimum(target * SLOTS + rank, targets * SLOTS - 1)
        out_ref[pl.ds(slot, 1)] = blocks_ref[pl.ds(block, 1)]


def place_blocks(dest, blocks, targets):
    whole = pl.BlockSpec(memory_space=pltpu.VMEM)
    shape = (targets * SLOTS,) + blocks.shape[1:]
    return pl.pallas_call(
        place_kernel,
        out_shape=jax.ShapeDtypeStruct(shape, blocks.dtype),
        in_specs=[pl.BlockSpec(memory_space=pltpu.SMEM), whole],
        out_specs=whole,
        scratch_shapes=[pltpu.SMEM((targets,), jnp.int32)],
        compiler_params=pltpu.CompilerParams(vmem_limit_bytes=16 << 20),
        cost_estimate=pl.CostEstimate(flops=0, bytes_accessed=6 * blocks.size, transcendentals=0),
        name="place_blocks",
    )(dest, blocks)


def project_kernel(place_ref, weight_ref, low_ref, high_ref, out_ref, rows, sums):
    shard, rank = place_ref[0], place_ref[1]
    ranks, count, _ = out_ref.shape
    _, total, wide = low_ref.shape
    pieces = rows.shape[1] // wide
    height = rows.shape[0] // (SIDE * SIDE)
    first = total - pieces * height
    for at in range(SIDE):
        for col in range(SIDE):
            held = (low_ref, high_ref)[at // 2]
            packed = held[at % 2 * SIDE + col, first:].astype(jnp.float32)
            start = ((at ^ (at // 2)) * SIDE + (col ^ (col // 2))) * height
            for piece in range(pieces):
                rows[start : start + height, piece * wide : (piece + 1) * wide] = packed[
                    piece * height : (piece + 1) * height, :
                ]
    sums[...] = dot(rows[...].astype(jnp.bfloat16), weight_ref[...])
    for other in range(ranks):
        pair = (rank ^ other) ^ (shard // 2)
        part = sums[pl.ds(pl.multiple_of(pair * count, count), count), :]
        swapped = jnp.concatenate([part[height:], part[:height]], axis=0)
        out_ref[other] = jnp.where(shard % 2 == 1, swapped, part)


def project(place, weight, low, high, ranks, steps):
    width = weight.shape[1]
    height = SIDE * SIDE * steps
    whole = pl.BlockSpec(memory_space=pltpu.VMEM)
    return pl.pallas_call(
        project_kernel,
        out_shape=jax.ShapeDtypeStruct((ranks, height // ranks, width), jnp.float32),
        in_specs=[pl.BlockSpec(memory_space=pltpu.SMEM)] + [whole] * 3,
        out_specs=whole,
        scratch_shapes=[
            pltpu.VMEM((height, weight.shape[0]), jnp.float32),
            pltpu.VMEM((height, width), jnp.float32),
        ],
        compiler_params=pltpu.CompilerParams(vmem_limit_bytes=16 << 20),
        cost_estimate=pl.CostEstimate(
            flops=2 * height * weight.size, bytes_accessed=2 * weight.size, transcendentals=0
        ),
        name="project",
    )(place, weight, low, high)


def exchange(value, axis, size, other):
    return lax.ppermute(value, axis, [(i, i ^ other) for i in range(size)])


def per_device(
    prompt_q, prompt_kv, sectioned, handoff_dest, dec_q, dec_new, cache, cache_len, output_weight
):
    shards = SIDE * SIDE
    shard = lax.axis_index("row") * SIDE + lax.axis_index("col")
    ranks = lax.axis_size("head")
    place = jnp.stack([shard, lax.axis_index("head")])

    near, far = first_step(cache_len, prompt_kv[0], dec_q[0], dec_new[0], cache[0])
    near, far = near[None], far[None]
    for other, axes in ((1, ("col", "row")), (3, ("col", "row")), (1, ("row", "col"))):
        near = jnp.concatenate([near, exchange(near, axes[0], SIDE, other)])
        far = jnp.concatenate([far, exchange(far, axes[1], SIDE, other)])
    near = [near, exchange(near, "row", SIDE, 3)]
    far = [far, exchange(far, "col", SIDE, 3)]

    other_dest = exchange(handoff_dest.reshape(1, -1), "grp", 2, 1)
    other_blocks = exchange(sectioned[0], "grp", 2, 1)
    outgoing = place_blocks(other_dest, other_blocks, shards)
    near, far, outgoing = lax.optimization_barrier((near, far, outgoing))
    arrived = lax.all_to_all(outgoing, ("row", "col"), 0, 0, tiled=True)

    sums = project(place, output_weight, *near, ranks, dec_q.shape[1] * dec_q.shape[2])
    while sums.shape[0] > 1:
        middle = sums.shape[0] // 2
        sums = sums[:middle] + exchange(sums[middle:], "head", ranks, middle)
    decode_out = sums[0].astype(jnp.bfloat16)
    prompt_attn = prompt_attention(place, prompt_q[0], near, far)
    return (prompt_attn[None], arrived[None], decode_out[None])


def solution(mesh):
    shape = mesh.shape
    grid = jax.sharding.Mesh(
        mesh.devices.reshape(shape["grp"], SIDE, SIDE, shape["head"]), ("grp", "row", "col", "head")
    )
    seq = ("row", "col")
    placed = (
        P("grp", seq, "head"),
        P("grp", seq, "head"),
        P("grp", seq, None, "head"),
        P("grp", seq, None),
        P("grp", seq, None, "head"),
        P("grp", seq, None, "head"),
        P("grp", seq, None, "head"),
        P("grp", seq),
        P("head", seq),
    )
    return jax.shard_map(
        per_device,
        mesh=grid,
        in_specs=placed,
        out_specs=(P("grp", seq, "head"), P("grp", seq, None, "head"), P("grp", "head", seq)),
        check_vma=False,
    )
```

```python
import math
from functools import partial

import jax
import jax.numpy as jnp
from jax import lax
from jax.experimental import pallas as pl
from jax.experimental.pallas import tpu as pltpu
from jax.sharding import PartitionSpec as P

QUERY_PER_KEY = 8
HEAD_WIDTH = 128
SCORE_SCALE = 1.0 / math.sqrt(HEAD_WIDTH)
EXP2_SCALE = SCORE_SCALE * math.log2(math.e)
LOWEST = -3.0e38
SLOTS = 4
SIDE = 4
EARLY = 3
TOP_LANE = HEAD_WIDTH + HEAD_WIDTH // 2

NT = (((1,), (1,)), ((), ()))
NN = (((1,), (0,)), ((), ()))


def dot(a, b, dims=NN):
    return lax.dot_general(a, b, dims, preferred_element_type=jnp.float32)


def gray(index):
    return index ^ (index // 2)


def prompt_kernel(outer, offset, kind, place_ref, q_ref, *refs):
    first, final = kind == "first", kind == "final"
    shard = place_ref[0]
    my_row, my_col = shard // SIDE, shard % SIDE
    if first:
        near_ref, far_ref, state_out, keys, key_cols, val = refs
        anchor_ref = near_ref
    elif final:
        anchor_ref, near_ref, far_ref, state_in, out_ref, keys, key_cols, val = refs[:8]
    else:
        anchor_ref, near_ref, far_ref, state_in, state_out, keys, key_cols, val = refs[:8]
    length = q_ref.shape[0]
    half = length // 2
    if kind in ("next", "final"):
        anchor, near, far, sems = refs[8:]
        copies = [
            pltpu.make_async_copy(anchor_ref.at[0:1, 0:16], anchor, sems.at[0]),
            pltpu.make_async_copy(near_ref.at[offset : offset + SIDE], near, sems.at[1]),
            pltpu.make_async_copy(far_ref.at[offset : offset + SIDE], far, sems.at[2]),
        ]
        for copy in copies:
            copy.start()
        for copy in copies:
            copy.wait()
        anchor_ref, near_ref, far_ref, offset = anchor, near, far, 0

    def run():
        own_key = jnp.broadcast_to(anchor_ref[0, :16, :HEAD_WIDTH][:1], (half, HEAD_WIDTH))
        for at in range(SIDE):
            for side, ref in enumerate((near_ref, far_ref)):
                part = ref[offset + at, :half]
                inner = gray(at)
                row, col = (my_row ^ outer, my_col ^ inner) if side == 0 else (my_row ^ inner, my_col ^ outer)
                seen = row * SIDE + col <= shard
                place = slice((2 * at + side) * half, (2 * at + side + 1) * half)
                keys[place, :] = jnp.where(seen, part[:, :HEAD_WIDTH], own_key)
                val[place, :HEAD_WIDTH] = jnp.where(seen, part[:, HEAD_WIDTH:], jnp.zeros_like(own_key))
                val[place, HEAD_WIDTH:] = jnp.where(seen, jnp.ones_like(own_key), jnp.zeros_like(own_key))
        turned = keys[...].T
        key_cols[:HEAD_WIDTH, :] = turned
        key_cols[HEAD_WIDTH:, :] = turned
        if first:
            masked = -(-length // HEAD_WIDTH) * HEAD_WIDTH
            spot = lax.broadcasted_iota(jnp.int32, (length, masked), 1)
            visible = (spot <= lax.broadcasted_iota(jnp.int32, (length, masked), 0)) | (spot >= length)

        lane = lax.broadcasted_iota(jnp.int32, (length, HEAD_WIDTH), 1)
        for head in range(QUERY_PER_KEY):
            rows = slice(head * length, (head + 1) * length)
            columns = slice(head * HEAD_WIDTH, (head + 1) * HEAD_WIDTH)
            scaled = q_ref[:, columns].astype(jnp.float32) * EXP2_SCALE
            high = scaled.astype(jnp.bfloat16)
            low = (scaled - high.astype(jnp.float32)).astype(jnp.bfloat16)
            scores = dot(jnp.concatenate([high, low], axis=1), key_cols[...])
            if first:
                scores = jnp.concatenate(
                    [jnp.where(visible, scores[:, :masked], LOWEST), scores[:, masked:]], axis=1
                )
            peak = jnp.max(scores, axis=1, keepdims=True)
            if not first:
                old = state_in[rows, TOP_LANE : TOP_LANE + 1]
                peak = jnp.maximum(old, peak)
            weights = jnp.exp2(scores - peak).astype(jnp.bfloat16)
            part = dot(weights, val[...])
            if not first:
                shrink = jnp.exp2(old - peak)
                total = state_in[rows, HEAD_WIDTH:]
                total = jnp.where(lane < TOP_LANE - HEAD_WIDTH, total, 0.0) * shrink + part[:, HEAD_WIDTH:]
                part = state_in[rows, :HEAD_WIDTH] * shrink + part[:, :HEAD_WIDTH]
            else:
                part, total = part[:, :HEAD_WIDTH], part[:, HEAD_WIDTH:]
            if final:
                out_ref[:, columns] = (part / total[:, :1]).astype(jnp.bfloat16)
            else:
                state_out[rows, :HEAD_WIDTH] = part
                state_out[rows, HEAD_WIDTH:] = jnp.where(lane < TOP_LANE - HEAD_WIDTH, total, peak)

    if kind == "ahead":
        pl.when(place_ref[1] < EARLY)(run)
    elif kind == "behind":
        pl.when(place_ref[1] >= EARLY)(run)
    else:
        run()


def prompt_part(place, outer, q, arrays, kind, state=None, offset=0):
    rows = QUERY_PER_KEY * q.shape[0]
    chunk = SIDE * q.shape[0]
    whole = pl.BlockSpec(memory_space=pltpu.VMEM)
    specs, fetched = [whole] * len(arrays), []
    if kind in ("next", "final"):
        arrays, specs = in_hbm(*arrays), [pl.BlockSpec(memory_space=pl.ANY)] * len(arrays)
        part = (SIDE,) + arrays[1].shape[1:]
        fetched = [
            pltpu.VMEM((1, 16, 2 * HEAD_WIDTH), jnp.bfloat16),
            pltpu.VMEM(part, jnp.bfloat16),
            pltpu.VMEM(part, jnp.bfloat16),
            pltpu.SemaphoreType.DMA((3,)),
        ]
    operands = arrays if state is None else (*arrays, state)
    specs = specs if state is None else specs + [whole]
    return pl.pallas_call(
        partial(prompt_kernel, outer, offset, kind),
        out_shape=jax.ShapeDtypeStruct(q.shape, jnp.bfloat16)
        if kind == "final"
        else pltpu.VMEM((rows, 2 * HEAD_WIDTH), jnp.float32),
        in_specs=[pl.BlockSpec(memory_space=pltpu.SMEM), whole] + specs,
        out_specs=whole,
        scratch_shapes=[
            pltpu.VMEM((chunk, HEAD_WIDTH), jnp.bfloat16),
            pltpu.VMEM((2 * HEAD_WIDTH, chunk), jnp.bfloat16),
            pltpu.VMEM((chunk, 2 * HEAD_WIDTH), jnp.bfloat16),
        ]
        + fetched,
        input_output_aliases={} if kind in ("first", "final") else {5: 0},
        compiler_params=pltpu.CompilerParams(vmem_limit_bytes=10 << 20),
        cost_estimate=pl.CostEstimate(
            flops=8 * rows * chunk * HEAD_WIDTH,
            bytes_accessed=4 * chunk * HEAD_WIDTH,
            transcendentals=rows * chunk,
        ),
        name="prompt_part",
    )(place, q, *operands)


def in_hbm(*arrays):
    return [pltpu.with_memory_space_constraint(array, pltpu.HBM) for array in arrays]


def first_kernel(len_hbm, kv_ref, q_ref, new_ref, cache_ref, near_ref, far_ref, *scratch):
    len_ref, kv, q_in, new_in, cache, q_rows, fresh, out_rows, packed, sems = scratch
    copies = [
        pltpu.make_async_copy(src, dst, sems.at[i])
        for i, (src, dst) in enumerate(
            ((cache_ref, cache), (kv_ref, kv), (q_ref, q_in), (new_ref, new_in), (len_hbm, len_ref))
        )
    ]
    for copy in copies:
        copy.start()
    requests, steps, _ = q_in.shape
    capacity = cache.shape[1]
    rows = QUERY_PER_KEY * steps
    half = far_ref.shape[0]
    fresh[...] = jnp.zeros_like(fresh)
    for copy in copies[1:]:
        copy.wait()
    near_ref[:half, :] = kv[:half, :]
    far_ref[...] = kv[half:, :]
    copies[0].wait()
    for req in range(requests):
        for head in range(QUERY_PER_KEY):
            q_rows[head * steps : (head + 1) * steps, :] = q_in[
                req, :, head * HEAD_WIDTH : (head + 1) * HEAD_WIDTH
            ].astype(jnp.float32)
        q = q_rows[...].astype(jnp.bfloat16)
        fresh[:steps, :] = new_in[req].astype(jnp.float32)
        new = fresh[...].astype(jnp.bfloat16)
        held = cache[req]
        scores = dot(q, held[:, :HEAD_WIDTH], NT)
        position = lax.broadcasted_iota(jnp.int32, (rows, capacity), 1)
        scores = jnp.where(position < len_ref[0, req], scores, LOWEST)
        new_scores = dot(q, new[:, :HEAD_WIDTH], NT)
        new_pos = lax.broadcasted_iota(jnp.int32, (rows, new.shape[0]), 1)
        step = lax.broadcasted_iota(jnp.int32, (rows, new.shape[0]), 0) % steps
        new_scores = jnp.where(new_pos <= step, new_scores, LOWEST)
        peak = jnp.maximum(
            jnp.max(scores, axis=1, keepdims=True), jnp.max(new_scores, axis=1, keepdims=True)
        )
        weights = jnp.exp2((scores - peak) * EXP2_SCALE)
        new_weights = jnp.exp2((new_scores - peak) * EXP2_SCALE)
        total = jnp.sum(weights, axis=1, keepdims=True) + jnp.sum(new_weights, axis=1, keepdims=True)
        summed = dot(weights.astype(jnp.bfloat16), held[:, HEAD_WIDTH:])
        summed = summed + dot(new_weights.astype(jnp.bfloat16), new[:, HEAD_WIDTH:])
        result = summed / total
        for head in range(QUERY_PER_KEY):
            out_rows[
                req * steps : (req + 1) * steps, head * HEAD_WIDTH : (head + 1) * HEAD_WIDTH
            ] = result[head * steps : (head + 1) * steps, :]
    height, wide = requests * steps, packed.shape[1]
    for piece in range(packed.shape[0] // height):
        packed[piece * height : (piece + 1) * height, :] = out_rows[
            :, piece * wide : (piece + 1) * wide
        ]
    near_ref[half:, :] = packed[...].astype(jnp.bfloat16)


def first_step(lengths, kv, q, new, cache):
    requests, steps, width = q.shape
    half, wide = kv.shape[0] // 2, kv.shape[1]
    height = requests * steps * width // wide
    whole = pl.BlockSpec(memory_space=pltpu.VMEM)
    far_off = pl.BlockSpec(memory_space=pl.ANY)
    return pl.pallas_call(
        first_kernel,
        out_shape=(
            pltpu.VMEM((half + height, wide), jnp.bfloat16),
            pltpu.VMEM((half, wide), jnp.bfloat16),
        ),
        in_specs=[far_off] * 5,
        out_specs=(whole, whole),
        scratch_shapes=[
            pltpu.SMEM(lengths.shape, jnp.int32),
            pltpu.VMEM(kv.shape, jnp.bfloat16),
            pltpu.VMEM(q.shape, jnp.bfloat16),
            pltpu.VMEM(new.shape, jnp.bfloat16),
            pltpu.VMEM(cache.shape, jnp.bfloat16),
            pltpu.VMEM((QUERY_PER_KEY * steps, HEAD_WIDTH), jnp.float32),
            pltpu.VMEM((HEAD_WIDTH, 2 * HEAD_WIDTH), jnp.float32),
            pltpu.VMEM((requests * steps, width), jnp.float32),
            pltpu.VMEM((height, wide), jnp.float32),
            pltpu.SemaphoreType.DMA((5,)),
        ],
        compiler_params=pltpu.CompilerParams(vmem_limit_bytes=16 << 20),
        cost_estimate=pl.CostEstimate(
            flops=4 * q.size * cache.shape[1], bytes_accessed=2 * cache.size, transcendentals=0
        ),
        name="first_step",
    )(*in_hbm(lengths, kv, q, new, cache))


def place_kernel(dest_hbm, blocks_hbm, out_ref, dest_ref, blocks_ref, count, sems):
    copies = [
        pltpu.make_async_copy(dest_hbm, dest_ref, sems.at[0]),
        pltpu.make_async_copy(blocks_hbm, blocks_ref, sems.at[1]),
    ]
    for copy in copies:
        copy.start()
    targets = out_ref.shape[0] // SLOTS
    for target in range(targets):
        count[target] = 0
    out_ref[...] = jnp.zeros_like(out_ref)
    for copy in copies:
        copy.wait()

    @pl.loop(0, blocks_ref.shape[0])
    def _(block):
        target = dest_ref[0, block]
        rank = count[target]
        count[target] = rank + 1
        slot = jnp.minimum(target * SLOTS + rank, targets * SLOTS - 1)
        out_ref[pl.ds(slot, 1)] = blocks_ref[pl.ds(block, 1)]


def place_blocks(dest, blocks, targets):
    shape = (targets * SLOTS,) + blocks.shape[1:]
    return pl.pallas_call(
        place_kernel,
        out_shape=jax.ShapeDtypeStruct(shape, blocks.dtype),
        in_specs=[pl.BlockSpec(memory_space=pl.ANY)] * 2,
        out_specs=pl.BlockSpec(memory_space=pltpu.VMEM),
        scratch_shapes=[
            pltpu.SMEM(dest.shape, jnp.int32),
            pltpu.VMEM(blocks.shape, blocks.dtype),
            pltpu.SMEM((targets,), jnp.int32),
            pltpu.SemaphoreType.DMA((2,)),
        ],
        compiler_params=pltpu.CompilerParams(vmem_limit_bytes=10 << 20),
        cost_estimate=pl.CostEstimate(flops=0, bytes_accessed=6 * blocks.size, transcendentals=0),
        name="place_blocks",
    )(*in_hbm(dest, blocks))


def project_kernel(place_ref, weight_ref, *refs):
    gathered, kept_ref, sent_ref, rows, sums = refs
    shard, rank = place_ref[0], place_ref[1]
    middle, count, _ = kept_ref.shape
    wide = gathered.shape[2]
    pieces = rows.shape[1] // wide
    height = rows.shape[0] // (SIDE * SIDE)
    for at in range(SIDE):
        for col in range(SIDE):
            packed = gathered[at * SIDE + col].astype(jnp.float32)
            start = (gray(at) * SIDE + gray(col)) * height
            for piece in range(pieces):
                rows[start : start + height, piece * wide : (piece + 1) * wide] = packed[
                    piece * height : (piece + 1) * height, :
                ]
    sums[...] = dot(rows[...].astype(jnp.bfloat16), weight_ref[...])
    for other in range(2 * middle):
        pair = (rank ^ other) ^ (shard // 2)
        part = sums[pl.ds(pl.multiple_of(pair * count, count), count), :]
        swapped = jnp.concatenate([part[height:], part[:height]], axis=0)
        part = jnp.where(shard % 2 == 1, swapped, part)
        if other < middle:
            kept_ref[other] = part
        else:
            sent_ref[other - middle] = part.astype(jnp.bfloat16)


def project(place, weight, gathered, ranks, steps):
    width = weight.shape[1]
    height = SIDE * SIDE * steps
    whole = pl.BlockSpec(memory_space=pltpu.VMEM)
    return pl.pallas_call(
        project_kernel,
        out_shape=(
            jax.ShapeDtypeStruct((ranks // 2, height // ranks, width), jnp.float32),
            jax.ShapeDtypeStruct((ranks // 2, height // ranks, width), jnp.bfloat16),
        ),
        in_specs=[pl.BlockSpec(memory_space=pltpu.SMEM)] + [whole] * 2,
        out_specs=(whole, whole),
        scratch_shapes=[
            pltpu.VMEM((height, weight.shape[0]), jnp.float32),
            pltpu.VMEM((height, width), jnp.float32),
        ],
        compiler_params=pltpu.CompilerParams(vmem_limit_bytes=16 << 20),
        cost_estimate=pl.CostEstimate(
            flops=2 * height * weight.size, bytes_accessed=2 * weight.size, transcendentals=0
        ),
        name="project",
    )(place, weight, gathered)


def exchange(value, axis, size, other):
    return lax.ppermute(value, axis, [(i, i ^ other) for i in range(size)])


def per_device(
    prompt_q, prompt_kv, sectioned, handoff_dest, dec_q, dec_new, cache, cache_len, output_weight
):
    shards = SIDE * SIDE
    shard = lax.axis_index("row") * SIDE + lax.axis_index("col")
    ranks = lax.axis_size("head")
    place = jnp.stack([shard, lax.axis_index("head")])
    q = prompt_q[0]
    half = prompt_kv.shape[1] // 2

    near, far = first_step(cache_len, prompt_kv[0], dec_q[0], dec_new[0], cache[0])
    near, far = near[None], far[None]
    near, far, blocks = lax.optimization_barrier((near, far, sectioned[0]))
    outgoing = place_blocks(handoff_dest.reshape(1, -1), blocks, shards)
    outgoing = exchange(outgoing, "grp", 2, 1)

    near = jnp.concatenate([near, exchange(near, "col", SIDE, 1)])
    far = jnp.concatenate([far, exchange(far, "row", SIDE, 1)])
    near_more, far_more = exchange(near, "col", SIDE, 3), exchange(far, "row", SIDE, 3)
    rows = jnp.concatenate([near[:, half:], near_more[:, half:]])
    near = jnp.concatenate([near[:, :half], near_more[:, :half]])
    far = jnp.concatenate([far, far_more])

    rows = jnp.concatenate([rows, exchange(rows, "row", SIDE, 1)])
    more = exchange(near, "row", SIDE, 1), exchange(far, "col", SIDE, 1)
    near, far, rows = lax.optimization_barrier((near, far, rows))
    rows = jnp.concatenate([rows, exchange(rows, "row", SIDE, 3)])
    state = prompt_part(place, 0, q, (near, far), "first")
    rows, more, state = lax.optimization_barrier((rows, more, state))
    wide = jnp.concatenate([near, more[0]]), jnp.concatenate([far, more[1]])
    last = exchange(wide[0], "row", SIDE, 3), exchange(wide[1], "col", SIDE, 3)

    steps = dec_q.shape[1] * dec_q.shape[2]
    sums, sent = project(place, output_weight, rows, ranks, steps)
    state = prompt_part(place, 1, q, (near, *more), "ahead", state)
    sums, sent, state = lax.optimization_barrier((sums, sent, state))
    sent = exchange(sent, "head", ranks, 4)
    state = prompt_part(place, 1, q, (near, *more), "behind", state)
    sent, last, state, outgoing = lax.optimization_barrier((sent, last, state, outgoing))
    arrived = lax.all_to_all(outgoing, ("row", "col"), 0, 0, tiled=True)

    sums = sums + sent.astype(jnp.float32)
    sums, state = lax.optimization_barrier((sums, state))
    sent = exchange(sums[2:], "head", ranks, 2)
    state = prompt_part(place, 3, q, (near, *last), "next", state)
    sent, state = lax.optimization_barrier((sent, state))
    sums = sums[:2] + sent
    sent = exchange(sums[1:], "head", ranks, 1)
    prompt_attn = prompt_part(place, 2, q, (near, *last), "final", state, offset=SIDE)
    sent, prompt_attn = lax.optimization_barrier((sent, prompt_attn))
    decode_out = (sums[0] + sent[0]).astype(jnp.bfloat16)
    return (prompt_attn[None], arrived[None], decode_out[None])


def solution(mesh):
    shape = mesh.shape
    grid = jax.sharding.Mesh(
        mesh.devices.reshape(shape["grp"], SIDE, SIDE, shape["head"]), ("grp", "row", "col", "head")
    )
    seq = ("row", "col")
    placed = (
        P("grp", seq, "head"),
        P("grp", seq, "head"),
        P("grp", seq, None, "head"),
        P("grp", seq, None),
        P("grp", seq, None, "head"),
        P("grp", seq, None, "head"),
        P("grp", seq, None, "head"),
        P("grp", seq),
        P("head", seq),
    )
    return jax.shard_map(
        per_device,
        mesh=grid,
        in_specs=placed,
        out_specs=(P("grp", seq, "head"), P("grp", seq, None, "head"), P("grp", "head", seq)),
        check_vma=False,
    )
```

```python
import math
from functools import partial

import jax
import jax.numpy as jnp
from jax import lax
from jax.experimental import pallas as pl
from jax.experimental.pallas import tpu as pltpu
from jax.sharding import PartitionSpec as P

QUERY_PER_KEY = 8
HEAD_WIDTH = 128
SCORE_SCALE = 1.0 / math.sqrt(HEAD_WIDTH)
EXP2_SCALE = SCORE_SCALE * math.log2(math.e)
LOWEST = -3.0e38
SLOTS = 4
SIDE = 4
EARLY = 3
TOP_LANE = HEAD_WIDTH + HEAD_WIDTH // 2

NT = (((1,), (1,)), ((), ()))
NN = (((1,), (0,)), ((), ()))


def dot(a, b, dims=NN):
    return lax.dot_general(a, b, dims, preferred_element_type=jnp.float32)


def gray(index):
    return index ^ (index // 2)


def prompt_kernel(outers, offset, kind, place_ref, q_ref, *refs):
    first, final = kind == "first", kind == "final"
    shard = place_ref[0]
    my_row, my_col = shard // SIDE, shard % SIDE
    if first:
        near_ref, far_ref, state_out, keys, key_cols, val = refs
        anchor_ref = near_ref
    elif final:
        anchor_ref, near_ref, far_ref, state_in, out_ref, keys, key_cols, val = refs[:8]
    else:
        anchor_ref, near_ref, far_ref, state_in, state_out, keys, key_cols, val = refs[:8]
    length = q_ref.shape[0]
    half = length // 2
    fetch = kind in ("behind", "final")
    if fetch:
        sources = near_ref, far_ref
        anchor, near_ref, far_ref, sems = refs[8:]
        count = near_ref.shape[0]
        copies = [pltpu.make_async_copy(anchor_ref.at[0:1, 0:16], anchor, sems.at[2])]
        for index, (source, held) in enumerate(zip(sources, (near_ref, far_ref))):
            part = source.at[offset : offset + count]
            copies.append(pltpu.make_async_copy(part, held, sems.at[index]))
        anchor_ref = anchor

    def run():
        if fetch:
            for copy in copies:
                copy.start()
            for copy in copies:
                copy.wait()
        own_key = jnp.broadcast_to(anchor_ref[0, :16, :HEAD_WIDTH][:1], (half, HEAD_WIDTH))
        for at in range(SIDE * len(outers)):
            for side, ref in enumerate((near_ref, far_ref)):
                part = ref[at, :half]
                outer, inner = outers[at // SIDE], gray(at % SIDE)
                row, col = (my_row ^ outer, my_col ^ inner) if side == 0 else (my_row ^ inner, my_col ^ outer)
                seen = row * SIDE + col <= shard
                place = slice((2 * at + side) * half, (2 * at + side + 1) * half)
                keys[place, :] = jnp.where(seen, part[:, :HEAD_WIDTH], own_key)
                val[place, :HEAD_WIDTH] = jnp.where(seen, part[:, HEAD_WIDTH:], jnp.zeros_like(own_key))
                val[place, HEAD_WIDTH:] = jnp.where(seen, jnp.ones_like(own_key), jnp.zeros_like(own_key))
        turned = keys[...].T
        key_cols[:HEAD_WIDTH, :] = turned
        key_cols[HEAD_WIDTH:, :] = turned
        if first:
            masked = -(-length // HEAD_WIDTH) * HEAD_WIDTH
            spot = lax.broadcasted_iota(jnp.int32, (length, masked), 1)
            visible = (spot <= lax.broadcasted_iota(jnp.int32, (length, masked), 0)) | (spot >= length)

        lane = lax.broadcasted_iota(jnp.int32, (length, HEAD_WIDTH), 1)
        for head in range(QUERY_PER_KEY):
            rows = slice(head * length, (head + 1) * length)
            columns = slice(head * HEAD_WIDTH, (head + 1) * HEAD_WIDTH)
            scaled = q_ref[:, columns].astype(jnp.float32) * EXP2_SCALE
            high = scaled.astype(jnp.bfloat16)
            low = (scaled - high.astype(jnp.float32)).astype(jnp.bfloat16)
            scores = dot(jnp.concatenate([high, low], axis=1), key_cols[...])
            if first:
                scores = jnp.concatenate(
                    [jnp.where(visible, scores[:, :masked], LOWEST), scores[:, masked:]], axis=1
                )
            peak = jnp.max(scores, axis=1, keepdims=True)
            if not first:
                old = state_in[rows, TOP_LANE : TOP_LANE + 1]
                peak = jnp.maximum(old, peak)
            weights = jnp.exp2(scores - peak).astype(jnp.bfloat16)
            part = dot(weights, val[...])
            if not first:
                shrink = jnp.exp2(old - peak)
                total = state_in[rows, HEAD_WIDTH:]
                total = jnp.where(lane < TOP_LANE - HEAD_WIDTH, total, 0.0) * shrink + part[:, HEAD_WIDTH:]
                part = state_in[rows, :HEAD_WIDTH] * shrink + part[:, :HEAD_WIDTH]
            else:
                part, total = part[:, :HEAD_WIDTH], part[:, HEAD_WIDTH:]
            if final:
                out_ref[:, columns] = (part / total[:, :1]).astype(jnp.bfloat16)
            else:
                state_out[rows, :HEAD_WIDTH] = part
                state_out[rows, HEAD_WIDTH:] = jnp.where(lane < TOP_LANE - HEAD_WIDTH, total, peak)

    if kind == "ahead":
        pl.when(place_ref[1] < EARLY)(run)
    elif kind == "behind":
        pl.when(place_ref[1] >= EARLY)(run)
    else:
        run()


def prompt_part(place, outers, q, arrays, kind, state=None, offset=0):
    rows = QUERY_PER_KEY * q.shape[0]
    chunk = SIDE * len(outers) * q.shape[0]
    whole = pl.BlockSpec(memory_space=pltpu.VMEM)
    specs, fetched = [whole] * len(arrays), []
    if kind in ("behind", "final"):
        arrays, specs = in_hbm(*arrays), [pl.BlockSpec(memory_space=pl.ANY)] * len(arrays)
        part = (SIDE * len(outers),) + arrays[1].shape[1:]
        fetched = [
            pltpu.VMEM((1, 16, 2 * HEAD_WIDTH), jnp.bfloat16),
            pltpu.VMEM(part, jnp.bfloat16),
            pltpu.VMEM(part, jnp.bfloat16),
            pltpu.SemaphoreType.DMA((3,)),
        ]
    operands = arrays if state is None else (*arrays, state)
    specs = specs if state is None else specs + [whole]
    return pl.pallas_call(
        partial(prompt_kernel, outers, offset, kind),
        out_shape=jax.ShapeDtypeStruct(q.shape, jnp.bfloat16)
        if kind == "final"
        else pltpu.VMEM((rows, 2 * HEAD_WIDTH), jnp.float32),
        in_specs=[pl.BlockSpec(memory_space=pltpu.SMEM), whole] + specs,
        out_specs=whole,
        scratch_shapes=[
            pltpu.VMEM((chunk, HEAD_WIDTH), jnp.bfloat16),
            pltpu.VMEM((2 * HEAD_WIDTH, chunk), jnp.bfloat16),
            pltpu.VMEM((chunk, 2 * HEAD_WIDTH), jnp.bfloat16),
        ]
        + fetched,
        input_output_aliases={} if kind in ("first", "final") else {5: 0},
        compiler_params=pltpu.CompilerParams(vmem_limit_bytes=12 << 20),
        cost_estimate=pl.CostEstimate(
            flops=(12 if kind == "final" else 8) * rows * chunk * HEAD_WIDTH,
            bytes_accessed=4 * chunk * HEAD_WIDTH,
            transcendentals=(12 if kind == "final" else 8) * rows * chunk // 8,
        ),
        name="prompt_part",
    )(place, q, *operands)


def in_hbm(*arrays):
    return [pltpu.with_memory_space_constraint(array, pltpu.HBM) for array in arrays]


def first_kernel(len_hbm, kv_ref, q_ref, new_ref, cache_ref, near_ref, far_ref, *scratch):
    len_ref, kv, q_in, new_in, cache, q_rows, fresh, out_rows, packed, sems = scratch
    copies = [
        pltpu.make_async_copy(src, dst, sems.at[i])
        for i, (src, dst) in enumerate(
            ((cache_ref, cache), (kv_ref, kv), (q_ref, q_in), (new_ref, new_in), (len_hbm, len_ref))
        )
    ]
    for copy in copies:
        copy.start()
    requests, steps, _ = q_in.shape
    capacity = cache.shape[1]
    rows = QUERY_PER_KEY * steps
    half = far_ref.shape[0]
    fresh[...] = jnp.zeros_like(fresh)
    for copy in copies[1:]:
        copy.wait()
    near_ref[:half, :] = kv[:half, :]
    far_ref[...] = kv[half:, :]
    copies[0].wait()
    for req in range(requests):
        for head in range(QUERY_PER_KEY):
            q_rows[head * steps : (head + 1) * steps, :] = q_in[
                req, :, head * HEAD_WIDTH : (head + 1) * HEAD_WIDTH
            ].astype(jnp.float32)
        q = q_rows[...].astype(jnp.bfloat16)
        fresh[:steps, :] = new_in[req].astype(jnp.float32)
        new = fresh[...].astype(jnp.bfloat16)
        held = cache[req]
        scores = dot(q, held[:, :HEAD_WIDTH], NT)
        position = lax.broadcasted_iota(jnp.int32, (rows, capacity), 1)
        scores = jnp.where(position < len_ref[0, req], scores, LOWEST)
        new_scores = dot(q, new[:, :HEAD_WIDTH], NT)
        new_pos = lax.broadcasted_iota(jnp.int32, (rows, new.shape[0]), 1)
        step = lax.broadcasted_iota(jnp.int32, (rows, new.shape[0]), 0) % steps
        new_scores = jnp.where(new_pos <= step, new_scores, LOWEST)
        peak = jnp.maximum(
            jnp.max(scores, axis=1, keepdims=True), jnp.max(new_scores, axis=1, keepdims=True)
        )
        weights = jnp.exp2((scores - peak) * EXP2_SCALE)
        new_weights = jnp.exp2((new_scores - peak) * EXP2_SCALE)
        total = jnp.sum(weights, axis=1, keepdims=True) + jnp.sum(new_weights, axis=1, keepdims=True)
        summed = dot(weights.astype(jnp.bfloat16), held[:, HEAD_WIDTH:])
        summed = summed + dot(new_weights.astype(jnp.bfloat16), new[:, HEAD_WIDTH:])
        result = summed / total
        for head in range(QUERY_PER_KEY):
            out_rows[
                req * steps : (req + 1) * steps, head * HEAD_WIDTH : (head + 1) * HEAD_WIDTH
            ] = result[head * steps : (head + 1) * steps, :]
    height, wide = requests * steps, packed.shape[1]
    for piece in range(packed.shape[0] // height):
        packed[piece * height : (piece + 1) * height, :] = out_rows[
            :, piece * wide : (piece + 1) * wide
        ]
    near_ref[half:, :] = packed[...].astype(jnp.bfloat16)


def first_step(lengths, kv, q, new, cache):
    requests, steps, width = q.shape
    half, wide = kv.shape[0] // 2, kv.shape[1]
    height = requests * steps * width // wide
    whole = pl.BlockSpec(memory_space=pltpu.VMEM)
    far_off = pl.BlockSpec(memory_space=pl.ANY)
    return pl.pallas_call(
        first_kernel,
        out_shape=(
            pltpu.VMEM((half + height, wide), jnp.bfloat16),
            pltpu.VMEM((half, wide), jnp.bfloat16),
        ),
        in_specs=[far_off] * 5,
        out_specs=(whole, whole),
        scratch_shapes=[
            pltpu.SMEM(lengths.shape, jnp.int32),
            pltpu.VMEM(kv.shape, jnp.bfloat16),
            pltpu.VMEM(q.shape, jnp.bfloat16),
            pltpu.VMEM(new.shape, jnp.bfloat16),
            pltpu.VMEM(cache.shape, jnp.bfloat16),
            pltpu.VMEM((QUERY_PER_KEY * steps, HEAD_WIDTH), jnp.float32),
            pltpu.VMEM((HEAD_WIDTH, 2 * HEAD_WIDTH), jnp.float32),
            pltpu.VMEM((requests * steps, width), jnp.float32),
            pltpu.VMEM((height, wide), jnp.float32),
            pltpu.SemaphoreType.DMA((5,)),
        ],
        compiler_params=pltpu.CompilerParams(vmem_limit_bytes=16 << 20),
        cost_estimate=pl.CostEstimate(
            flops=4 * q.size * cache.shape[1], bytes_accessed=2 * cache.size, transcendentals=0
        ),
        name="first_step",
    )(*in_hbm(lengths, kv, q, new, cache))


def place_kernel(dest_hbm, blocks_hbm, out_ref, dest_ref, blocks_ref, count, sems):
    copies = [
        pltpu.make_async_copy(dest_hbm, dest_ref, sems.at[0]),
        pltpu.make_async_copy(blocks_hbm, blocks_ref, sems.at[1]),
    ]
    for copy in copies:
        copy.start()
    targets = out_ref.shape[0] // SLOTS
    for target in range(targets):
        count[target] = 0
    out_ref[...] = jnp.zeros_like(out_ref)
    for copy in copies:
        copy.wait()

    @pl.loop(0, blocks_ref.shape[0])
    def _(block):
        target = dest_ref[0, block]
        rank = count[target]
        count[target] = rank + 1
        slot = jnp.minimum(target * SLOTS + rank, targets * SLOTS - 1)
        out_ref[pl.ds(slot, 1)] = blocks_ref[pl.ds(block, 1)]


def place_blocks(dest, blocks, targets):
    shape = (targets * SLOTS,) + blocks.shape[1:]
    return pl.pallas_call(
        place_kernel,
        out_shape=jax.ShapeDtypeStruct(shape, blocks.dtype),
        in_specs=[pl.BlockSpec(memory_space=pl.ANY)] * 2,
        out_specs=pl.BlockSpec(memory_space=pltpu.VMEM),
        scratch_shapes=[
            pltpu.SMEM(dest.shape, jnp.int32),
            pltpu.VMEM(blocks.shape, blocks.dtype),
            pltpu.SMEM((targets,), jnp.int32),
            pltpu.SemaphoreType.DMA((2,)),
        ],
        compiler_params=pltpu.CompilerParams(vmem_limit_bytes=10 << 20),
        cost_estimate=pl.CostEstimate(flops=0, bytes_accessed=6 * blocks.size, transcendentals=0),
        name="place_blocks",
    )(*in_hbm(dest, blocks))


def project_kernel(place_ref, weight_ref, *refs):
    gathered, kept_ref, sent_ref, rows, sums = refs
    shard, rank = place_ref[0], place_ref[1]
    middle, count, _ = kept_ref.shape
    wide = gathered.shape[2]
    pieces = rows.shape[1] // wide
    height = rows.shape[0] // (SIDE * SIDE)
    for at in range(SIDE):
        for col in range(SIDE):
            packed = gathered[at * SIDE + col].astype(jnp.float32)
            start = (gray(at) * SIDE + gray(col)) * height
            for piece in range(pieces):
                rows[start : start + height, piece * wide : (piece + 1) * wide] = packed[
                    piece * height : (piece + 1) * height, :
                ]
    sums[...] = dot(rows[...].astype(jnp.bfloat16), weight_ref[...])
    for other in range(2 * middle):
        pair = (rank ^ other) ^ (shard // 2)
        part = sums[pl.ds(pl.multiple_of(pair * count, count), count), :]
        swapped = jnp.concatenate([part[height:], part[:height]], axis=0)
        part = jnp.where(shard % 2 == 1, swapped, part)
        if other < middle:
            kept_ref[other] = part
        else:
            sent_ref[other - middle] = part.astype(jnp.bfloat16)


def project(place, weight, gathered, ranks, steps):
    width = weight.shape[1]
    height = SIDE * SIDE * steps
    whole = pl.BlockSpec(memory_space=pltpu.VMEM)
    return pl.pallas_call(
        project_kernel,
        out_shape=(
            jax.ShapeDtypeStruct((ranks // 2, height // ranks, width), jnp.float32),
            jax.ShapeDtypeStruct((ranks // 2, height // ranks, width), jnp.bfloat16),
        ),
        in_specs=[pl.BlockSpec(memory_space=pltpu.SMEM)] + [whole] * 2,
        out_specs=(whole, whole),
        scratch_shapes=[
            pltpu.VMEM((height, weight.shape[0]), jnp.float32),
            pltpu.VMEM((height, width), jnp.float32),
        ],
        compiler_params=pltpu.CompilerParams(vmem_limit_bytes=16 << 20),
        cost_estimate=pl.CostEstimate(
            flops=2 * height * weight.size, bytes_accessed=2 * weight.size, transcendentals=0
        ),
        name="project",
    )(place, weight, gathered)


def mark_kernel(value_ref, out_ref):
    out_ref[...] = jnp.zeros_like(out_ref)


def mark(value):
    return pl.pallas_call(
        mark_kernel,
        out_shape=jax.ShapeDtypeStruct((8, HEAD_WIDTH), jnp.float32),
        in_specs=[pl.BlockSpec(memory_space=pl.ANY)],
        out_specs=pl.BlockSpec(memory_space=pltpu.VMEM),
        cost_estimate=pl.CostEstimate(flops=1 << 33, bytes_accessed=1 << 12, transcendentals=0),
        name="mark",
    )(value)


def join_kernel(*refs):
    parts, outs, sems = refs[:4], refs[4:6], refs[6]
    copies = []
    for index, part in enumerate(parts):
        count = part.shape[0]
        place = outs[index // 2].at[pl.ds(index % 2 * count, count)]
        copies.append(pltpu.make_async_copy(part, place, sems.at[index]))
    for copy in copies:
        copy.start()
    for copy in copies:
        copy.wait()


def join(first, second):
    whole = pl.BlockSpec(memory_space=pltpu.VMEM)
    shape = (2 * first[0].shape[0],) + first[0].shape[1:]
    return pl.pallas_call(
        join_kernel,
        out_shape=[pltpu.HBM(shape, first[0].dtype)] * 2,
        in_specs=[whole] * 4,
        out_specs=[pl.BlockSpec(memory_space=pl.ANY)] * 2,
        scratch_shapes=[pltpu.SemaphoreType.DMA((4,))],
        compiler_params=pltpu.CompilerParams(vmem_limit_bytes=4 << 20),
        name="join",
    )(*first, *second)


def exchange(value, axis, size, other):
    return lax.ppermute(value, axis, [(i, i ^ other) for i in range(size)])


def per_device(
    prompt_q, prompt_kv, sectioned, handoff_dest, dec_q, dec_new, cache, cache_len, output_weight
):
    shards = SIDE * SIDE
    shard = lax.axis_index("row") * SIDE + lax.axis_index("col")
    ranks = lax.axis_size("head")
    place = jnp.stack([shard, lax.axis_index("head")])
    q = prompt_q[0]
    half = prompt_kv.shape[1] // 2

    near, far = first_step(cache_len, prompt_kv[0], dec_q[0], dec_new[0], cache[0])
    near, far = near[None], far[None]
    near, far, blocks = lax.optimization_barrier((near, far, sectioned[0]))
    outgoing = place_blocks(handoff_dest.reshape(1, -1), blocks, shards)
    outgoing = exchange(outgoing, "grp", 2, 1)

    near = jnp.concatenate([near, exchange(near, "col", SIDE, 1)])
    far = jnp.concatenate([far, exchange(far, "row", SIDE, 1)])
    near_more, far_more = exchange(near, "col", SIDE, 3), exchange(far, "row", SIDE, 3)
    rows = jnp.concatenate([near[:, half:], near_more[:, half:]])
    near = jnp.concatenate([near[:, :half], near_more[:, :half]])
    far = jnp.concatenate([far, far_more])

    rows = jnp.concatenate([rows, exchange(rows, "row", SIDE, 1)])
    more = exchange(near, "row", SIDE, 1), exchange(far, "col", SIDE, 1)
    near, far, rows = lax.optimization_barrier((near, far, rows))
    rows = jnp.concatenate([rows, exchange(rows, "row", SIDE, 3)])
    state = prompt_part(place, (0,), q, (near, far), "first")
    rows, more, state = lax.optimization_barrier((rows, more, state))
    wide = join((near, more[0]), (far, more[1]))
    last = exchange(wide[0], "row", SIDE, 3), exchange(wide[1], "col", SIDE, 3)

    steps = dec_q.shape[1] * dec_q.shape[2]
    sums, sent = project(place, output_weight, rows, ranks, steps)
    state = prompt_part(place, (1,), q, (near, *more), "ahead", state)
    near, far = wide
    sums, sent, state = lax.optimization_barrier((sums, sent, state))
    token = mark(sums)
    sent = exchange(sent, "head", ranks, 4)
    token, outgoing = lax.optimization_barrier((token, outgoing))
    arrived = lax.all_to_all(outgoing, ("row", "col"), 0, 0, tiled=True)

    sums = sums + sent.astype(jnp.float32)
    sums, near, far, state = lax.optimization_barrier((sums, near, far, state))
    sent = exchange(sums[2:], "head", ranks, 2)
    state = prompt_part(place, (1,), q, (near, near, far), "behind", state, offset=SIDE)
    sent, last, state = lax.optimization_barrier((sent, last, state))
    sums = sums[:2] + sent
    sent = exchange(sums[1:], "head", ranks, 1)
    prompt_attn = prompt_part(place, (3, 2), q, (near, *last), "final", state)
    sent, prompt_attn = lax.optimization_barrier((sent, prompt_attn))
    decode_out = (sums[0] + sent[0]).astype(jnp.bfloat16)
    return (prompt_attn[None], arrived[None], decode_out[None])


def solution(mesh):
    shape = mesh.shape
    grid = jax.sharding.Mesh(
        mesh.devices.reshape(shape["grp"], SIDE, SIDE, shape["head"]), ("grp", "row", "col", "head")
    )
    seq = ("row", "col")
    placed = (
        P("grp", seq, "head"),
        P("grp", seq, "head"),
        P("grp", seq, None, "head"),
        P("grp", seq, None),
        P("grp", seq, None, "head"),
        P("grp", seq, None, "head"),
        P("grp", seq, None, "head"),
        P("grp", seq),
        P("head", seq),
    )
    return jax.shard_map(
        per_device,
        mesh=grid,
        in_specs=placed,
        out_specs=(P("grp", seq, "head"), P("grp", seq, None, "head"), P("grp", "head", seq)),
        check_vma=False,
    )
```

```python
import math
from functools import partial

import jax
import jax.numpy as jnp
from jax import lax
from jax.experimental import pallas as pl
from jax.experimental.pallas import tpu as pltpu
from jax.sharding import PartitionSpec as P

QUERY_PER_KEY = 8
HEAD_WIDTH = 128
SCORE_SCALE = 1.0 / math.sqrt(HEAD_WIDTH)
EXP2_SCALE = SCORE_SCALE * math.log2(math.e)
LOWEST = -3.0e38
SLOTS = 4
SIDE = 4
EARLY = 3
TOP_LANE = HEAD_WIDTH + HEAD_WIDTH // 2

NT = (((1,), (1,)), ((), ()))
NN = (((1,), (0,)), ((), ()))


def dot(a, b, dims=NN):
    return lax.dot_general(a, b, dims, preferred_element_type=jnp.float32)


def gray(index):
    return index ^ (index // 2)


def prompt_kernel(outers, offset, kind, place_ref, q_ref, *refs):
    first, final = kind == "first", kind == "final"
    shard = place_ref[0]
    my_row, my_col = shard // SIDE, shard % SIDE
    if first:
        near_ref, far_ref, state_out, keys, key_cols, val = refs
        anchor_ref = near_ref
    elif final:
        anchor_ref, near_ref, far_ref, state_in, out_ref, keys, key_cols, val = refs[:8]
    else:
        anchor_ref, near_ref, far_ref, state_in, state_out, keys, key_cols, val = refs[:8]
    length = q_ref.shape[0]
    half = length // 2
    fetch = kind in ("behind", "final")
    if fetch:
        sources = near_ref, far_ref
        anchor, near_ref, far_ref, sems = refs[8:]
        count = near_ref.shape[0]
        copies = [pltpu.make_async_copy(anchor_ref.at[0:1, 0:16], anchor, sems.at[2])]
        for index, (source, held) in enumerate(zip(sources, (near_ref, far_ref))):
            part = source.at[offset : offset + count]
            copies.append(pltpu.make_async_copy(part, held, sems.at[index]))
        anchor_ref = anchor

    def run():
        if fetch:
            for copy in copies:
                copy.start()
            for copy in copies[:2]:
                copy.wait()
        own_key = jnp.broadcast_to(anchor_ref[0, :16, :HEAD_WIDTH][:1], (half, HEAD_WIDTH))
        for side, ref in enumerate((near_ref, far_ref)):
            if fetch and side == 1:
                copies[2].wait()
            for at in range(SIDE * len(outers)):
                part = ref[at, :half]
                outer, inner = outers[at // SIDE], gray(at % SIDE)
                row, col = (my_row ^ outer, my_col ^ inner) if side == 0 else (my_row ^ inner, my_col ^ outer)
                seen = row * SIDE + col <= shard
                place = slice((2 * at + side) * half, (2 * at + side + 1) * half)
                keys[place, :] = jnp.where(seen, part[:, :HEAD_WIDTH], own_key)
                val[place, :HEAD_WIDTH] = jnp.where(seen, part[:, HEAD_WIDTH:], jnp.zeros_like(own_key))
                val[place, HEAD_WIDTH:] = jnp.where(seen, jnp.ones_like(own_key), jnp.zeros_like(own_key))
        turned = keys[...].T
        key_cols[:HEAD_WIDTH, :] = turned
        key_cols[HEAD_WIDTH:, :] = turned
        if first:
            masked = -(-length // HEAD_WIDTH) * HEAD_WIDTH
            spot = lax.broadcasted_iota(jnp.int32, (length, masked), 1)
            visible = (spot <= lax.broadcasted_iota(jnp.int32, (length, masked), 0)) | (spot >= length)

        lane = lax.broadcasted_iota(jnp.int32, (length, HEAD_WIDTH), 1)
        for head in range(QUERY_PER_KEY):
            rows = slice(head * length, (head + 1) * length)
            columns = slice(head * HEAD_WIDTH, (head + 1) * HEAD_WIDTH)
            scaled = q_ref[:, columns].astype(jnp.float32) * EXP2_SCALE
            high = scaled.astype(jnp.bfloat16)
            low = (scaled - high.astype(jnp.float32)).astype(jnp.bfloat16)
            scores = dot(jnp.concatenate([high, low], axis=1), key_cols[...])
            if first:
                scores = jnp.concatenate(
                    [jnp.where(visible, scores[:, :masked], LOWEST), scores[:, masked:]], axis=1
                )
            peak = jnp.max(scores, axis=1, keepdims=True)
            if not first:
                old = state_in[rows, TOP_LANE : TOP_LANE + 1]
                peak = jnp.maximum(old, peak)
            weights = jnp.exp2(scores - peak).astype(jnp.bfloat16)
            part = dot(weights, val[...])
            if not first:
                shrink = jnp.exp2(old - peak)
                total = state_in[rows, HEAD_WIDTH:]
                total = jnp.where(lane < TOP_LANE - HEAD_WIDTH, total, 0.0) * shrink + part[:, HEAD_WIDTH:]
                part = state_in[rows, :HEAD_WIDTH] * shrink + part[:, :HEAD_WIDTH]
            else:
                part, total = part[:, :HEAD_WIDTH], part[:, HEAD_WIDTH:]
            if final:
                out_ref[:, columns] = (part / total[:, :1]).astype(jnp.bfloat16)
            else:
                state_out[rows, :HEAD_WIDTH] = part
                state_out[rows, HEAD_WIDTH:] = jnp.where(lane < TOP_LANE - HEAD_WIDTH, total, peak)

    if kind == "ahead":
        pl.when(place_ref[1] < EARLY)(run)
    elif kind == "behind":
        pl.when(place_ref[1] >= EARLY)(run)
    else:
        run()


def prompt_part(place, outers, q, arrays, kind, state=None, offset=0):
    rows = QUERY_PER_KEY * q.shape[0]
    chunk = SIDE * len(outers) * q.shape[0]
    whole = pl.BlockSpec(memory_space=pltpu.VMEM)
    specs, fetched = [whole] * len(arrays), []
    if kind in ("behind", "final"):
        arrays, specs = in_hbm(*arrays), [pl.BlockSpec(memory_space=pl.ANY)] * len(arrays)
        part = (SIDE * len(outers),) + arrays[1].shape[1:]
        fetched = [
            pltpu.VMEM((1, 16, 2 * HEAD_WIDTH), jnp.bfloat16),
            pltpu.VMEM(part, jnp.bfloat16),
            pltpu.VMEM(part, jnp.bfloat16),
            pltpu.SemaphoreType.DMA((3,)),
        ]
    operands = arrays if state is None else (*arrays, state)
    specs = specs if state is None else specs + [whole]
    return pl.pallas_call(
        partial(prompt_kernel, outers, offset, kind),
        out_shape=jax.ShapeDtypeStruct(q.shape, jnp.bfloat16)
        if kind == "final"
        else pltpu.VMEM((rows, 2 * HEAD_WIDTH), jnp.float32),
        in_specs=[pl.BlockSpec(memory_space=pltpu.SMEM), whole] + specs,
        out_specs=whole,
        scratch_shapes=[
            pltpu.VMEM((chunk, HEAD_WIDTH), jnp.bfloat16),
            pltpu.VMEM((2 * HEAD_WIDTH, chunk), jnp.bfloat16),
            pltpu.VMEM((chunk, 2 * HEAD_WIDTH), jnp.bfloat16),
        ]
        + fetched,
        input_output_aliases={} if kind in ("first", "final") else {5: 0},
        compiler_params=pltpu.CompilerParams(vmem_limit_bytes=12 << 20),
        cost_estimate=pl.CostEstimate(
            flops=(12 if kind == "final" else 8) * rows * chunk * HEAD_WIDTH,
            bytes_accessed=4 * chunk * HEAD_WIDTH,
            transcendentals=(12 if kind == "final" else 8) * rows * chunk // 8,
        ),
        name="prompt_part",
    )(place, q, *operands)


def in_hbm(*arrays):
    return [pltpu.with_memory_space_constraint(array, pltpu.HBM) for array in arrays]


def first_kernel(len_hbm, kv_ref, q_ref, new_ref, cache_ref, near_ref, far_ref, *scratch):
    len_ref, kv, q_in, new_in, cache, q_rows, fresh, out_rows, packed, sems = scratch
    pairs = [(kv_ref, kv), (q_ref, q_in), (new_ref, new_in), (len_hbm, len_ref)]
    pairs += [(cache_ref.at[req], cache.at[req]) for req in range(q_in.shape[0])]
    copies = [
        pltpu.make_async_copy(src, dst, sems.at[i])
        for i, (src, dst) in enumerate(
            pairs
        )
    ]
    for copy in copies:
        copy.start()
    requests, steps, _ = q_in.shape
    capacity = cache.shape[1]
    rows = QUERY_PER_KEY * steps
    half = far_ref.shape[0]
    fresh[...] = jnp.zeros_like(fresh)
    for copy in copies[:4]:
        copy.wait()
    near_ref[:half, :] = kv[:half, :]
    far_ref[...] = kv[half:, :]
    for req in range(requests):
        copies[4 + req].wait()
        for head in range(QUERY_PER_KEY):
            q_rows[head * steps : (head + 1) * steps, :] = q_in[
                req, :, head * HEAD_WIDTH : (head + 1) * HEAD_WIDTH
            ].astype(jnp.float32)
        q = q_rows[...].astype(jnp.bfloat16)
        fresh[:steps, :] = new_in[req].astype(jnp.float32)
        new = fresh[...].astype(jnp.bfloat16)
        held = cache[req]
        scores = dot(q, held[:, :HEAD_WIDTH], NT)
        position = lax.broadcasted_iota(jnp.int32, (rows, capacity), 1)
        scores = jnp.where(position < len_ref[0, req], scores, LOWEST)
        new_scores = dot(q, new[:, :HEAD_WIDTH], NT)
        new_pos = lax.broadcasted_iota(jnp.int32, (rows, new.shape[0]), 1)
        step = lax.broadcasted_iota(jnp.int32, (rows, new.shape[0]), 0) % steps
        new_scores = jnp.where(new_pos <= step, new_scores, LOWEST)
        peak = jnp.maximum(
            jnp.max(scores, axis=1, keepdims=True), jnp.max(new_scores, axis=1, keepdims=True)
        )
        weights = jnp.exp2((scores - peak) * EXP2_SCALE)
        new_weights = jnp.exp2((new_scores - peak) * EXP2_SCALE)
        total = jnp.sum(weights, axis=1, keepdims=True) + jnp.sum(new_weights, axis=1, keepdims=True)
        summed = dot(weights.astype(jnp.bfloat16), held[:, HEAD_WIDTH:])
        summed = summed + dot(new_weights.astype(jnp.bfloat16), new[:, HEAD_WIDTH:])
        result = summed / total
        for head in range(QUERY_PER_KEY):
            out_rows[
                req * steps : (req + 1) * steps, head * HEAD_WIDTH : (head + 1) * HEAD_WIDTH
            ] = result[head * steps : (head + 1) * steps, :]
    height, wide = requests * steps, packed.shape[1]
    for piece in range(packed.shape[0] // height):
        packed[piece * height : (piece + 1) * height, :] = out_rows[
            :, piece * wide : (piece + 1) * wide
        ]
    near_ref[half:, :] = packed[...].astype(jnp.bfloat16)


def first_step(lengths, kv, q, new, cache):
    requests, steps, width = q.shape
    half, wide = kv.shape[0] // 2, kv.shape[1]
    height = requests * steps * width // wide
    whole = pl.BlockSpec(memory_space=pltpu.VMEM)
    far_off = pl.BlockSpec(memory_space=pl.ANY)
    return pl.pallas_call(
        first_kernel,
        out_shape=(
            pltpu.VMEM((half + height, wide), jnp.bfloat16),
            pltpu.VMEM((half, wide), jnp.bfloat16),
        ),
        in_specs=[far_off] * 5,
        out_specs=(whole, whole),
        scratch_shapes=[
            pltpu.SMEM(lengths.shape, jnp.int32),
            pltpu.VMEM(kv.shape, jnp.bfloat16),
            pltpu.VMEM(q.shape, jnp.bfloat16),
            pltpu.VMEM(new.shape, jnp.bfloat16),
            pltpu.VMEM(cache.shape, jnp.bfloat16),
            pltpu.VMEM((QUERY_PER_KEY * steps, HEAD_WIDTH), jnp.float32),
            pltpu.VMEM((HEAD_WIDTH, 2 * HEAD_WIDTH), jnp.float32),
            pltpu.VMEM((requests * steps, width), jnp.float32),
            pltpu.VMEM((height, wide), jnp.float32),
            pltpu.SemaphoreType.DMA((4 + requests,)),
        ],
        compiler_params=pltpu.CompilerParams(vmem_limit_bytes=16 << 20),
        cost_estimate=pl.CostEstimate(
            flops=4 * q.size * cache.shape[1], bytes_accessed=2 * cache.size, transcendentals=0
        ),
        name="first_step",
    )(*in_hbm(lengths, kv, q, new, cache))


def place_kernel(dest_hbm, blocks_hbm, out_ref, dest_ref, blocks_ref, count, sems):
    copies = [
        pltpu.make_async_copy(dest_hbm, dest_ref, sems.at[0]),
        pltpu.make_async_copy(blocks_hbm, blocks_ref, sems.at[1]),
    ]
    for copy in copies:
        copy.start()
    targets = out_ref.shape[0] // SLOTS
    for target in range(targets):
        count[target] = 0
    out_ref[...] = jnp.zeros_like(out_ref)
    for copy in copies:
        copy.wait()

    @pl.loop(0, blocks_ref.shape[0])
    def _(block):
        target = dest_ref[0, block]
        rank = count[target]
        count[target] = rank + 1
        slot = jnp.minimum(target * SLOTS + rank, targets * SLOTS - 1)
        out_ref[pl.ds(slot, 1)] = blocks_ref[pl.ds(block, 1)]


def place_blocks(dest, blocks, targets):
    shape = (targets * SLOTS,) + blocks.shape[1:]
    return pl.pallas_call(
        place_kernel,
        out_shape=jax.ShapeDtypeStruct(shape, blocks.dtype),
        in_specs=[pl.BlockSpec(memory_space=pl.ANY)] * 2,
        out_specs=pl.BlockSpec(memory_space=pltpu.VMEM),
        scratch_shapes=[
            pltpu.SMEM(dest.shape, jnp.int32),
            pltpu.VMEM(blocks.shape, blocks.dtype),
            pltpu.SMEM((targets,), jnp.int32),
            pltpu.SemaphoreType.DMA((2,)),
        ],
        compiler_params=pltpu.CompilerParams(vmem_limit_bytes=10 << 20),
        cost_estimate=pl.CostEstimate(flops=0, bytes_accessed=6 * blocks.size, transcendentals=0),
        name="place_blocks",
    )(*in_hbm(dest, blocks))


def project_kernel(place_ref, weight_ref, *refs):
    gathered, kept_ref, sent_ref, rows, sums = refs
    shard, rank = place_ref[0], place_ref[1]
    middle, count, _ = kept_ref.shape
    wide = gathered.shape[2]
    pieces = rows.shape[1] // wide
    height = rows.shape[0] // (SIDE * SIDE)
    for at in range(SIDE):
        for col in range(SIDE):
            packed = gathered[at * SIDE + col].astype(jnp.float32)
            start = (gray(at) * SIDE + gray(col)) * height
            for piece in range(pieces):
                rows[start : start + height, piece * wide : (piece + 1) * wide] = packed[
                    piece * height : (piece + 1) * height, :
                ]
    sums[...] = dot(rows[...].astype(jnp.bfloat16), weight_ref[...])
    for other in range(2 * middle):
        pair = (rank ^ other) ^ (shard // 2)
        part = sums[pl.ds(pl.multiple_of(pair * count, count), count), :]
        swapped = jnp.concatenate([part[height:], part[:height]], axis=0)
        part = jnp.where(shard % 2 == 1, swapped, part)
        if other < middle:
            kept_ref[other] = part
        else:
            sent_ref[other - middle] = part.astype(jnp.bfloat16)


def project(place, weight, gathered, ranks, steps):
    width = weight.shape[1]
    height = SIDE * SIDE * steps
    whole = pl.BlockSpec(memory_space=pltpu.VMEM)
    return pl.pallas_call(
        project_kernel,
        out_shape=(
            jax.ShapeDtypeStruct((ranks // 2, height // ranks, width), jnp.float32),
            jax.ShapeDtypeStruct((ranks // 2, height // ranks, width), jnp.bfloat16),
        ),
        in_specs=[pl.BlockSpec(memory_space=pltpu.SMEM)] + [whole] * 2,
        out_specs=(whole, whole),
        scratch_shapes=[
            pltpu.VMEM((height, weight.shape[0]), jnp.float32),
            pltpu.VMEM((height, width), jnp.float32),
        ],
        compiler_params=pltpu.CompilerParams(vmem_limit_bytes=16 << 20),
        cost_estimate=pl.CostEstimate(
            flops=2 * height * weight.size, bytes_accessed=2 * weight.size, transcendentals=0
        ),
        name="project",
    )(place, weight, gathered)


def mark_kernel(value_ref, out_ref):
    out_ref[...] = jnp.zeros_like(out_ref)


def mark(value):
    return pl.pallas_call(
        mark_kernel,
        out_shape=jax.ShapeDtypeStruct((8, HEAD_WIDTH), jnp.float32),
        in_specs=[pl.BlockSpec(memory_space=pl.ANY)],
        out_specs=pl.BlockSpec(memory_space=pltpu.VMEM),
        cost_estimate=pl.CostEstimate(flops=1 << 33, bytes_accessed=1 << 12, transcendentals=0),
        name="mark",
    )(value)


def join_kernel(*refs):
    parts, outs, sems = refs[:4], refs[4:6], refs[6]
    copies = []
    for index, part in enumerate(parts):
        count = part.shape[0]
        place = outs[index // 2].at[pl.ds(index % 2 * count, count)]
        copies.append(pltpu.make_async_copy(part, place, sems.at[index]))
    for copy in copies:
        copy.start()
    for copy in copies:
        copy.wait()


def join(first, second):
    whole = pl.BlockSpec(memory_space=pltpu.VMEM)
    shape = (2 * first[0].shape[0],) + first[0].shape[1:]
    return pl.pallas_call(
        join_kernel,
        out_shape=[pltpu.HBM(shape, first[0].dtype)] * 2,
        in_specs=[whole] * 4,
        out_specs=[pl.BlockSpec(memory_space=pl.ANY)] * 2,
        scratch_shapes=[pltpu.SemaphoreType.DMA((4,))],
        compiler_params=pltpu.CompilerParams(vmem_limit_bytes=4 << 20),
        name="join",
    )(*first, *second)


def exchange(value, axis, size, other):
    return lax.ppermute(value, axis, [(i, i ^ other) for i in range(size)])


def per_device(
    prompt_q, prompt_kv, sectioned, handoff_dest, dec_q, dec_new, cache, cache_len, output_weight
):
    shards = SIDE * SIDE
    shard = lax.axis_index("row") * SIDE + lax.axis_index("col")
    ranks = lax.axis_size("head")
    place = jnp.stack([shard, lax.axis_index("head")])
    q = prompt_q[0]
    half = prompt_kv.shape[1] // 2

    near, far = first_step(cache_len, prompt_kv[0], dec_q[0], dec_new[0], cache[0])
    near, far = near[None], far[None]
    near, far, blocks = lax.optimization_barrier((near, far, sectioned[0]))
    outgoing = place_blocks(handoff_dest.reshape(1, -1), blocks, shards)
    outgoing = exchange(outgoing, "grp", 2, 1)

    near = jnp.concatenate([near, exchange(near, "col", SIDE, 1)])
    far = jnp.concatenate([far, exchange(far, "row", SIDE, 1)])
    near_more, far_more = exchange(near, "col", SIDE, 3), exchange(far, "row", SIDE, 3)
    rows = jnp.concatenate([near[:, half:], near_more[:, half:]])
    near = jnp.concatenate([near[:, :half], near_more[:, :half]])
    far = jnp.concatenate([far, far_more])

    rows = jnp.concatenate([rows, exchange(rows, "row", SIDE, 1)])
    more = exchange(near, "row", SIDE, 1), exchange(far, "col", SIDE, 1)
    near, far, rows = lax.optimization_barrier((near, far, rows))
    rows = jnp.concatenate([rows, exchange(rows, "row", SIDE, 3)])
    state = prompt_part(place, (0,), q, (near, far), "first")
    rows, more, state = lax.optimization_barrier((rows, more, state))
    wide = join((near, more[0]), (far, more[1]))
    last = exchange(wide[0], "row", SIDE, 3), exchange(wide[1], "col", SIDE, 3)

    steps = dec_q.shape[1] * dec_q.shape[2]
    sums, sent = project(place, output_weight, rows, ranks, steps)
    state = prompt_part(place, (1,), q, (near, *more), "ahead", state)
    near, far = wide
    sums, sent, state = lax.optimization_barrier((sums, sent, state))
    token = mark(sums)
    sent = exchange(sent, "head", ranks, 4)
    token, outgoing = lax.optimization_barrier((token, outgoing))
    arrived = lax.all_to_all(outgoing, ("row", "col"), 0, 0, tiled=True)

    sums = sums + sent.astype(jnp.float32)
    sums, near, far, state = lax.optimization_barrier((sums, near, far, state))
    sent = exchange(sums[2:], "head", ranks, 2)
    state = prompt_part(place, (1,), q, (near, near, far), "behind", state, offset=SIDE)
    sent, last, state = lax.optimization_barrier((sent, last, state))
    sums = sums[:2] + sent
    sent = exchange(sums[1:], "head", ranks, 1)
    prompt_attn = prompt_part(place, (3, 2), q, (near, *last), "final", state)
    sent, prompt_attn = lax.optimization_barrier((sent, prompt_attn))
    decode_out = (sums[0] + sent[0]).astype(jnp.bfloat16)
    return (prompt_attn[None], arrived[None], decode_out[None])


def solution(mesh):
    shape = mesh.shape
    grid = jax.sharding.Mesh(
        mesh.devices.reshape(shape["grp"], SIDE, SIDE, shape["head"]), ("grp", "row", "col", "head")
    )
    seq = ("row", "col")
    placed = (
        P("grp", seq, "head"),
        P("grp", seq, "head"),
        P("grp", seq, None, "head"),
        P("grp", seq, None),
        P("grp", seq, None, "head"),
        P("grp", seq, None, "head"),
        P("grp", seq, None, "head"),
        P("grp", seq),
        P("head", seq),
    )
    return jax.shard_map(
        per_device,
        mesh=grid,
        in_specs=placed,
        out_specs=(P("grp", seq, "head"), P("grp", seq, None, "head"), P("grp", "head", seq)),
        check_vma=False,
    )
```
